32 devices in a mesh: dcn: 2 (over core), gx: 4 (over z), gy: 4 (over y, x).
Axes of the slice: x: 2, y: 2, z: 4, core: 2. Of those that a mesh axis runs over, the one named last changes fastest.
Arguments:
- features: bfloat16 [2, 64, 64, 2, 8, 128], P('dcn', 'gx', 'gy'), may hold values from -6 to 6
- grad_out: bfloat16 [2, 64, 64, 2, 8, 128], P('dcn', 'gx', 'gy'), may hold values from -6 to 6
- occupancy: int32 [2, 64, 64, 2, 8], P('dcn', 'gx', 'gy'), may hold values from 0 to 1, as said below
- leaf_z: int32 [2, 8, 8, 2], P('dcn', 'gx', 'gy'), may hold values from -1 to 2, as said below
- neighbours: int32 [2, 8, 8, 2, 27], P('dcn', 'gx', 'gy'), may hold values from 0 to 2, as said below
- kernel: bfloat16 [27, 128, 128], replicated, may hold values from -0.15625 to 0.15625
Outputs:
- grad_features: bfloat16 [2, 64, 64, 2, 8, 128], P('dcn', 'gx', 'gy')
- kernel_grad: float32 [27, 128, 128], replicated
The draws below stay inside these ranges and needn't reach their ends.
Inputs may be any that keep to these rules, and one draw needn't show every extreme that they name: `leaf_z`: in every leaf column the active slots come first, with distinct z positions in rising order below 3; the other slots hold -1. Every scene has a leaf column with all 2 slots active. `neighbours`: for an active slot holding z position h and offset k = 9 (p + 1) + 3 (q + 1) + (r + 1), the slot of the active leaf at z position h + r in the column p, q away, or 2 if there is none; slots that are not active hold 2 at every offset. `occupancy`: zero at every voxel of a slot that is not active.
All inputs are finite; a program needn't handle non-finite values.
Results may differ from the reference program's by a relative error of at most 0.001.
Values may be sent and summed in bfloat16 or wider, within the bound.
A program may use at most 64 MiB of HBM per device.

```python
import math
import jax
import jax.numpy as jnp
from jax import lax

C = 128
EDGE = 8
LEAVES = 2
DEPTH = 3
SCENES = 2
TILES_X = 8
TILES_Y = 8
NX = 64
NY = 64


def layout_tables(key):
    seeded = jax.random.fold_in(key, 4051)
    key_count, key_full, key_perm, key_mask = jax.random.split(seeded, 4)
    tile_count = SCENES * TILES_X * TILES_Y
    picked = jax.random.randint(key_count, (SCENES, TILES_X, TILES_Y), 0, LEAVES)
    filled = 1 + picked * picked // LEAVES
    full_tile = jax.random.randint(key_full, (SCENES,), 0, TILES_X * TILES_Y)
    tile_ids = jnp.arange(TILES_X * TILES_Y, dtype=jnp.int32).reshape(TILES_X, TILES_Y)
    filled = jnp.where(tile_ids[None] == full_tile[:, None, None], LEAVES, filled)
    perms = jax.vmap(lambda subkey: jax.random.permutation(subkey, DEPTH))(jax.random.split(key_perm, tile_count))
    perms = perms.reshape(SCENES, TILES_X, TILES_Y, DEPTH).astype(jnp.int32)
    slot_ids = jnp.arange(LEAVES, dtype=jnp.int32)
    filled_slot = slot_ids < filled[..., None]
    chosen = jnp.where(filled_slot, perms[..., :LEAVES], DEPTH + slot_ids)
    chosen = jnp.sort(chosen, axis=-1)
    leaf_z = jnp.where(filled_slot, chosen, -1).astype(jnp.int32)
    padded = jnp.pad(leaf_z, ((0, 0), (1, 1), (1, 1), (0, 0)), constant_values=-1)
    adjacent = []
    for step_x in (-1, 0, 1):
        for step_y in (-1, 0, 1):
            beside = padded[:, 1 + step_x:1 + step_x + TILES_X, 1 + step_y:1 + step_y + TILES_Y]
            for step_z in (-1, 0, 1):
                equals = (beside[..., None, :] == leaf_z[..., :, None] + step_z) & (beside[..., None, :] >= 0) & (leaf_z[..., :, None] >= 0)
                exists = jnp.any(equals, axis=-1)
                located = jnp.sum(jnp.where(equals, slot_ids, 0), axis=-1)
                adjacent.append(jnp.where(exists, located, LEAVES))
    neighbours = jnp.stack(adjacent, axis=-1).astype(jnp.int32)
    coin_flip = jax.random.randint(key_mask, (SCENES, NX, NY, LEAVES, EDGE), 0, 2)
    live_vox = jnp.repeat(jnp.repeat(filled_slot.astype(jnp.int32), EDGE, axis=1), EDGE, axis=2)
    occupancy = (coin_flip * live_vox[..., None]).astype(jnp.int32)
    return (leaf_z, neighbours, occupancy)


def draw_occupancy(key, part):
    return layout_tables(key)[2]


def draw_leaf_z(key, part):
    return layout_tables(key)[0]


def draw_neighbours(key, part):
    return layout_tables(key)[1]


def steps_of(key, extent, cuts, least, largest):
    level, own = 1.0, jax.random.fold_in(key, 6)
    for dim, parts in cuts:
        steps = jnp.exp(jax.random.uniform(jax.random.fold_in(own, dim), (parts,), jnp.float32, least / len(cuts), largest / len(cuts)))
        level = level * jnp.repeat(steps, extent[dim] // parts).reshape([-1 if axis == dim else 1 for axis in range(len(extent))])
    return level


def centred(stream_key, shape, deviation, limit, cuts=(), held_as=jnp.bfloat16):
    values = deviation * jax.random.normal(stream_key, shape, jnp.float32)
    if cuts:
        values = values * steps_of(stream_key, shape, cuts, -0.22, 0.18)
    return jnp.clip(values, -limit, limit).astype(held_as)


def setup_inputs(seed: int = 0) -> dict:
    streams_of = jax.random.split(jax.random.key(seed), 7)
    features = centred(streams_of[0], (SCENES, NX, NY, LEAVES, EDGE, C), 1.0, 6.0, ((0, 2), (1, 4), (2, 4)))
    grad_out = centred(streams_of[1], (SCENES, NX, NY, LEAVES, EDGE, C), 1.0, 6.0, ((0, 2), (1, 4), (2, 4)))
    occupancy = draw_occupancy(jax.random.fold_in(streams_of[6], 71), 0)
    leaf_z = draw_leaf_z(jax.random.fold_in(streams_of[6], 71), 0)
    neighbours = draw_neighbours(jax.random.fold_in(streams_of[6], 71), 0)
    kernel = centred(streams_of[5], (27, C, C), (27 * C // 2) ** -0.5, 0.15625)
    return {"features": features, "grad_out": grad_out, "occupancy": occupancy, "leaf_z": leaf_z, "neighbours": neighbours, "kernel": kernel}


def leaf_columns(padded, adjacent_row, edge):
    width = padded.shape[-1]
    spots = jnp.arange(edge + 2, dtype=jnp.int32)
    region = (spots > 0).astype(jnp.int32) + (spots > edge).astype(jnp.int32)
    base_index = region[:, None] * 9 + region[None, :] * 3
    rows_x = spots[:, None]
    rows_y = spots[None, :]
    planes = []
    for layer in range(3):
        chosen_slot = jnp.take(adjacent_row, base_index + layer)
        planes.append(padded[rows_x, rows_y, chosen_slot])
    column = jnp.concatenate([planes[0][:, :, edge - 1:], planes[1], planes[2][:, :, :1]], axis=2)
    pieces = []
    for step_x in (-1, 0, 1):
        for step_y in (-1, 0, 1):
            for step_z in (-1, 0, 1):
                pieces.append(column[1 - step_x:1 - step_x + edge, 1 - step_y:1 - step_y + edge, 1 - step_z:1 - step_z + edge])
    stacked = jnp.stack(pieces, axis=3)
    return stacked.reshape(edge * edge * edge, 27 * width)

def tile_terms(halo_zero, masked_in, keep, adjacent, active_total, wrows):
    edge = masked_in.shape[0]
    leaves = masked_in.shape[2]
    width = masked_in.shape[-1]

    def one_leaf(leaf, carry):
        grad_tile, kernel_acc = carry
        columns = leaf_columns(halo_zero, adjacent[leaf], edge)
        own = lax.dynamic_index_in_dim(masked_in, leaf, 2, keepdims=False).reshape(edge * edge * edge, width)
        leaf_keep = lax.dynamic_index_in_dim(keep, leaf, 2, keepdims=False).reshape(edge * edge * edge)
        result = jnp.dot(columns, wrows, preferred_element_type=jnp.float32) * leaf_keep[:, None].astype(jnp.float32)
        grad_tile = lax.dynamic_update_slice_in_dim(grad_tile, result.astype(jnp.bfloat16).reshape(edge, edge, 1, edge, width), leaf, 2)
        kernel_acc = kernel_acc + jnp.dot(own.T, columns, preferred_element_type=jnp.float32)
        return (grad_tile, kernel_acc)
    start = (jnp.zeros((edge, edge, leaves, edge, width), jnp.bfloat16), jnp.zeros((width, 27 * width), jnp.float32))
    return lax.fori_loop(0, active_total, one_leaf, start)

def reference(features, grad_out, occupancy, leaf_z, neighbours, kernel):
    active = (leaf_z >= 0).astype(jnp.int32)
    active_vox = jnp.repeat(jnp.repeat(active, EDGE, axis=1), EDGE, axis=2)
    keep = occupancy * active_vox[..., None]
    keep_b = keep.astype(jnp.bfloat16)[..., None]
    masked = grad_out * keep_b
    masked_in = features * keep_b
    padded = jnp.pad(masked, ((0, 0), (1, 1), (1, 1), (0, 0), (0, 0), (0, 0)))
    padded = jnp.concatenate([padded, jnp.zeros((SCENES, NX + 2, NY + 2, 1, EDGE, C), jnp.bfloat16)], axis=3)
    wrows = jnp.transpose(kernel, (0, 2, 1)).reshape(27 * C, C)
    totals = lax.optimization_barrier(jnp.sum(active, axis=-1)).astype(jnp.int32)

    def per_tile(kernel_sum, tile):
        scene = tile // (TILES_X * TILES_Y)
        tile_x = tile // TILES_Y % TILES_X
        tile_y = tile % TILES_Y
        nought = jnp.zeros((), jnp.int32)
        halo_zero = lax.dynamic_slice(padded, (scene, tile_x * EDGE, tile_y * EDGE, nought, nought, nought), (1, EDGE + 2, EDGE + 2, LEAVES + 1, EDGE, C))[0]
        own_in = lax.dynamic_slice(masked_in, (scene, tile_x * EDGE, tile_y * EDGE, nought, nought, nought), (1, EDGE, EDGE, LEAVES, EDGE, C))[0]
        own_keep = lax.dynamic_slice(keep, (scene, tile_x * EDGE, tile_y * EDGE, nought, nought), (1, EDGE, EDGE, LEAVES, EDGE))[0]
        adjacent = neighbours[scene, tile_x, tile_y]
        grad_tile, kernel_part = tile_terms(halo_zero, own_in, own_keep, adjacent, totals[scene, tile_x, tile_y], wrows)
        return (kernel_sum + kernel_part, grad_tile)
    tiles = jnp.arange(SCENES * TILES_X * TILES_Y, dtype=jnp.int32)
    kernel_sum, grads = lax.scan(per_tile, jnp.zeros((C, 27 * C), jnp.float32), tiles)
    grads = grads.reshape(SCENES, TILES_X, TILES_Y, EDGE, EDGE, LEAVES, EDGE, C)
    grads = jnp.transpose(grads, (0, 1, 3, 2, 4, 5, 6, 7)).reshape(SCENES, NX, NY, LEAVES, EDGE, C)
    scale = 1.0 / math.sqrt(SCENES * NX * NY * LEAVES * EDGE)
    kernel_grad = jnp.transpose(kernel_sum.reshape(C, 27, C), (1, 0, 2)) * scale
    return (grads, kernel_grad)
```

```python
import functools
import math

import jax
import jax.numpy as jnp
from jax import lax
from jax.experimental import pallas as pl
from jax.experimental.pallas import tpu as pltpu
from jax.sharding import PartitionSpec as P

MESH = pl.DeviceIdType.MESH
BF16 = jnp.bfloat16
F32 = jnp.float32


def padded_2(cells, sides):
    for axis, dim in sides:
        count = lax.axis_size(axis)
        ends = count - 1
        head = lax.slice_in_dim(cells, 0, 1, axis=dim)
        tail = lax.slice_in_dim(cells, cells.shape[dim] - 1, cells.shape[dim], axis=dim)
        cells = jnp.concatenate(
            [
                lax.ppermute(tail, axis, [(i, (i + 1) % count) for i in range(ends)]),
                cells,
                lax.ppermute(head, axis, [((i + 1) % count, i) for i in range(ends)]),
            ],
            axis=dim,
        )
    return cells


def leaf_kernel(cols_y, leaves, edge, leaf_z, dense, own_in, wrows, grad, kacc, patches):
    step = pl.program_id(0)
    wide = edge + 2
    width = wrows.shape[-1]
    plane = edge * edge
    rows = edge * plane

    @pl.when(step == 0)
    def _():
        kacc[...] = jnp.zeros_like(kacc)

    height = leaf_z[step]
    column = step // leaves
    x0 = (column // cols_y) * edge
    y0 = pl.multiple_of((column % cols_y) * plane, plane)

    @pl.when(height >= 0)
    def _():
        def window(position):
            block = dense[position, pl.ds(x0, wide), pl.ds(y0, wide * edge), :]
            return block.astype(F32).reshape(wide * wide, edge, width)

        low, mid, high = window(height), window(height + 1), window(height + 2)
        spot = lax.broadcasted_iota(jnp.int32, low.shape, 1)
        shifted = (
            jnp.where(spot == edge - 1, pltpu.roll(high, edge - 1, 1), pltpu.roll(mid, edge - 1, 1)),
            mid,
            jnp.where(spot == 0, pltpu.roll(low, 1, 1), pltpu.roll(mid, 1, 1)),
        )
        for c in range(3):
            cells = shifted[c].reshape(wide, wide, edge, width)
            for b in range(3):
                piece = cells[:, 2 - b : 2 - b + edge].reshape(wide * plane, width)
                lane = (3 * b + c) * width
                patches[:, lane : lane + width] = piece.astype(BF16)
        own_t = own_in[0].astype(F32).T.astype(BF16)
        result = jnp.zeros((rows, width), F32)
        for a in range(3):
            columns = patches[(2 - a) * plane : (2 - a) * plane + rows, :]
            result += jnp.dot(
                columns,
                wrows[9 * a * width : 9 * (a + 1) * width, :],
                preferred_element_type=F32,
            )
            terms = jnp.dot(own_t, columns, preferred_element_type=F32)
            for j in range(9):
                row = (9 * a + j) * width
                kacc[row : row + width, :] += terms[:, j * width : (j + 1) * width]
        grad[0] = result.astype(BF16)


def reduce_kernel(sizes, scale, acc, out, half_buf, half_sum, gy_buf, gy_sum, gx_buf, send, recv):
    n_dcn, n_gx, n_gy = sizes
    dcn, gx, gy = (lax.axis_index(name) for name in ("dcn", "gx", "gy"))
    per = gx_buf.shape[1]
    quarter = per * n_gx
    half = quarter * n_gy

    def dcn_peer(d):
        return lax.rem(dcn + d, n_dcn)

    def gy_peer(d):
        return lax.rem(gy + d, n_gy)

    def gx_peer(d):
        return lax.rem(gx + d, n_gx)

    barrier = pltpu.get_barrier_semaphore()
    peers = (
        [(dcn_peer(d), gx, gy) for d in range(1, n_dcn)]
        + [(dcn, gx, gy_peer(d)) for d in range(1, n_gy)]
        + [(dcn, gx_peer(d), gy) for d in range(1, n_gx)]
    )
    for peer in peers:
        pl.semaphore_signal(barrier, inc=1, device_id=peer, device_id_type=MESH)
    pl.semaphore_wait(barrier, len(peers))

    used = [0]

    def copy(src, dst, device):
        slot = used[0]
        used[0] += 1
        made = pltpu.make_async_remote_copy(
            src_ref=src,
            dst_ref=dst,
            send_sem=send.at[slot],
            recv_sem=recv.at[slot],
            device_id=device,
            device_id_type=MESH,
        )
        made.start()
        return made

    def span(start, size):
        return pl.ds(pl.multiple_of(start, 8), size)

    copies = [
        copy(acc.at[span(dcn_peer(d) * half, half)], half_buf.at[d - 1], (dcn_peer(d), gx, gy))
        for d in range(1, n_dcn)
    ]
    for made in copies:
        made.wait()
    total = acc[span(dcn * half, half), :]
    for d in range(1, n_dcn):
        total += half_buf[d - 1]
    half_sum[...] = total

    copies = [
        copy(
            half_sum.at[span(gy_peer(d) * quarter, quarter)],
            gy_buf.at[d - 1],
            (dcn, gx, gy_peer(d)),
        )
        for d in range(1, n_gy)
    ]
    for made in copies:
        made.wait()
    total = half_sum[span(gy * quarter, quarter), :]
    for d in range(1, n_gy):
        total += gy_buf[d - 1]
    gy_sum[...] = total

    copies = [
        copy(gy_sum.at[span(gx_peer(d) * per, per)], gx_buf.at[d - 1], (dcn, gx_peer(d), gy))
        for d in range(1, n_gx)
    ]
    for made in copies:
        made.wait()
    total = gy_sum[span(gx * per, per), :]
    for d in range(1, n_gx):
        total += gx_buf[d - 1]
    mine = span(dcn * half + gy * quarter + gx * per, per)
    out[mine, :] = total * scale

    copies = [
        copy(out.at[mine], out.at[mine], (dcn, gx_peer(d), gy)) for d in range(1, n_gx)
    ]
    for made in copies:
        made.wait()
    mine = span(dcn * half + gy * quarter, quarter)
    copies = [
        copy(out.at[mine], out.at[mine], (dcn, gx, gy_peer(d))) for d in range(1, n_gy)
    ]
    for made in copies:
        made.wait()
    mine = span(dcn * half, half)
    copies = [
        copy(out.at[mine], out.at[mine], (dcn_peer(d), gx, gy)) for d in range(1, n_dcn)
    ]
    for made in copies:
        made.wait()


def local(features, grad_out, occupancy, leaf_z, neighbours, kernel):
    edge = features.shape[4]
    leaves = features.shape[3]
    width = features.shape[-1]
    cols_x = leaf_z.shape[1]
    cols_y = leaf_z.shape[2]
    depth = 3
    voxels = edge * edge * edge
    sizes = tuple(lax.axis_size(name) for name in ("dcn", "gx", "gy"))
    devices = sizes[0] * sizes[1] * sizes[2]
    slots = cols_x * cols_y * leaves
    nx, ny = cols_x * edge, cols_y * edge

    heights = jnp.repeat(jnp.repeat(leaf_z[0], edge, axis=0), edge, axis=1)
    keep = occupancy[0] * (heights >= 0).astype(jnp.int32)[..., None]
    placed = jnp.stack([keep * (heights == z).astype(jnp.int32)[..., None] for z in range(depth)])
    dense = sum(
        grad_out[0][None, :, :, slot] * placed[:, :, :, slot].astype(BF16)[..., None]
        for slot in range(leaves)
    )
    halo = padded_2(dense, (("gx", 1), ("gy", 2)))
    halo = jnp.pad(halo, ((1, 1), (0, 0), (0, 0), (0, 0), (0, 0)))
    halo = halo.reshape(depth + 2, nx + 2, (ny + 2) * edge, width)
    masked_in = features[0] * keep.astype(BF16)[..., None]
    own = masked_in.reshape(cols_x, edge, cols_y, edge, leaves, edge, width)
    own = own.transpose(0, 2, 4, 1, 3, 5, 6).reshape(slots, voxels, width)
    wrows = jnp.transpose(kernel, (0, 2, 1)).reshape(27 * width, width)

    per = -(-27 * width // (devices * 8)) * 8
    total_rows = per * devices
    whole = lambda *shape: pl.BlockSpec(shape, lambda i, z: (0,) * len(shape))
    grads, kacc = pl.pallas_call(
        functools.partial(leaf_kernel, cols_y, leaves, edge),
        grid_spec=pltpu.PrefetchScalarGridSpec(
            num_scalar_prefetch=1,
            grid=(slots,),
            in_specs=[
                whole(*halo.shape),
                pl.BlockSpec((1, voxels, width), lambda i, z: (i, 0, 0)),
                whole(*wrows.shape),
            ],
            out_specs=[
                pl.BlockSpec((1, voxels, width), lambda i, z: (i, 0, 0)),
                whole(total_rows, width),
            ],
            scratch_shapes=[pltpu.VMEM(((edge + 2) * edge * edge, 9 * width), BF16)],
        ),
        out_shape=[
            jax.ShapeDtypeStruct((slots, voxels, width), BF16),
            jax.ShapeDtypeStruct((total_rows, width), F32),
        ],
        compiler_params=pltpu.CompilerParams(vmem_limit_bytes=40 * 2**20),
        cost_estimate=pl.CostEstimate(
            flops=4 * slots * voxels * 27 * width * width,
            bytes_accessed=8 * 2**20,
            transcendentals=0,
        ),
    )(leaf_z.reshape(slots), halo, own, wrows)

    scale = 1.0 / math.sqrt(devices * cols_x * cols_y * voxels * leaves)
    half = total_rows // sizes[0]
    quarter = half // sizes[2]
    count = 2 * (sum(sizes) - 3)
    vmem = pl.BlockSpec(memory_space=pltpu.VMEM)
    kernel_grad = pl.pallas_call(
        functools.partial(reduce_kernel, sizes, scale),
        out_shape=jax.ShapeDtypeStruct((total_rows, width), F32),
        in_specs=[vmem],
        out_specs=vmem,
        scratch_shapes=[
            pltpu.VMEM((sizes[0] - 1, half, width), F32),
            pltpu.VMEM((half, width), F32),
            pltpu.VMEM((sizes[2] - 1, quarter, width), F32),
            pltpu.VMEM((quarter, width), F32),
            pltpu.VMEM((sizes[1] - 1, per, width), F32),
            pltpu.SemaphoreType.DMA((count,)),
            pltpu.SemaphoreType.DMA((count,)),
        ],
        compiler_params=pltpu.CompilerParams(
            collective_id=0, has_side_effects=True, vmem_limit_bytes=40 * 2**20
        ),
    )(kacc)
    kernel_grad = kernel_grad[: 27 * width].reshape(27, width, width)

    block = grads.reshape(cols_x, cols_y, leaves, edge, edge, edge, width)
    block = block.transpose(0, 3, 1, 4, 2, 5, 6).reshape(nx, ny, leaves, edge, width)
    block = jnp.where(keep[..., None] > 0, block, jnp.zeros((), BF16))
    return (block[None], kernel_grad)


def solution(mesh):
    return jax.shard_map(
        local,
        mesh=mesh,
        in_specs=(
            P("dcn", "gx", "gy", None, None, None),
            P("dcn", "gx", "gy", None, None, None),
            P("dcn", "gx", "gy", None, None),
            P("dcn", "gx", "gy", None),
            P("dcn", "gx", "gy", None, None),
            P(),
        ),
        out_specs=(P("dcn", "gx", "gy", None, None, None), P()),
        check_vma=False,
    )
```

```python
import functools
import math

import jax
import jax.numpy as jnp
from jax import lax
from jax.experimental import pallas as pl
from jax.experimental.pallas import tpu as pltpu
from jax.sharding import PartitionSpec as P

MESH = pl.DeviceIdType.MESH
BF16 = jnp.bfloat16
F32 = jnp.float32


def sides_of(sizes):
    n_gx, n_gy = sizes[1:]
    gx, gy = lax.axis_index("gx"), lax.axis_index("gy")
    sides = []
    for dx in (-1, 0, 1):
        for dy in (-1, 0, 1):
            if dx or dy:
                x, y = gx + dx, gy + dy
                inside = (x >= 0) & (x < n_gx) & (y >= 0) & (y < n_gy)
                sides.append((dx, dy, x, y, inside))
    return sides


def halo_kernel(sizes, cols, leaf_z, grad_out, keep, kernel, dense, wrows, send, recv):
    cols_x, cols_y = cols
    leaves, edge, width = grad_out.shape[2:]
    depth = dense.shape[0]
    voxels = edge * edge * edge
    extent = (cols_x * edge, cols_y * edge)
    dcn = lax.axis_index("dcn")
    sides = sides_of(sizes)
    barrier = pltpu.get_barrier_semaphore()
    for dx, dy, x, y, inside in sides:

        @pl.when(inside)
        def _():
            pl.semaphore_signal(barrier, inc=1, device_id=(dcn, x, y), device_id_type=MESH)

    for cx in range(cols_x):
        for cy in range(cols_y):
            masked = []
            for leaf in range(leaves):
                slot = (cx * cols_y + cy) * leaves + leaf
                cells = grad_out[
                    cx * edge : (cx + 1) * edge, cy * edge : (cy + 1) * edge, leaf
                ].astype(F32)
                kept = jnp.broadcast_to(keep[slot], (width, voxels)).T
                masked.append((leaf_z[slot], cells * kept.reshape(edge, edge, edge, width)))
            for z in range(depth):
                placed = sum(
                    jnp.where(height == z, cells, jnp.zeros_like(cells))
                    for height, cells in masked
                )
                dense[
                    z,
                    1 + cx * edge : 1 + (cx + 1) * edge,
                    1 + cy * edge : 1 + (cy + 1) * edge,
                ] = placed.astype(BF16)

    def source(step, size):
        return {-1: pl.ds(1, 1), 0: pl.ds(1, size), 1: pl.ds(size, 1)}[step]

    def target(step, size):
        return {-1: pl.ds(size + 1, 1), 0: pl.ds(1, size), 1: pl.ds(0, 1)}[step]

    def copy_to(index):
        dx, dy, x, y, _ = sides[index]
        return pltpu.make_async_remote_copy(
            src_ref=dense.at[:, source(dx, extent[0]), source(dy, extent[1])],
            dst_ref=dense.at[:, target(dx, extent[0]), target(dy, extent[1])],
            send_sem=send.at[index],
            recv_sem=recv.at[index],
            device_id=(dcn, x, y),
            device_id_type=MESH,
        )

    pl.semaphore_wait(barrier, sum(inside.astype(jnp.int32) for *_, inside in sides))

    for index, (dx, dy, x, y, inside) in enumerate(sides):

        @pl.when(inside)
        def _():
            copy_to(index).start()

        @pl.when(jnp.logical_not(inside))
        def _():
            ends = []
            for step, size in ((dx, extent[0]), (dy, extent[1])):
                ends.append({-1: slice(0, 1), 0: slice(1, size + 1), 1: slice(size + 1, size + 2)}[step])
            spot = dense.at[:, ends[0], ends[1]]
            spot[...] = jnp.zeros(spot.shape, BF16)

    for k in range(kernel.shape[0]):
        wrows[k * width : (k + 1) * width, :] = kernel[k].astype(F32).T.astype(BF16)

    for index in range(len(sides)):

        @pl.when(sides[index][4])
        def _():
            copy_to(index).wait_send()

        @pl.when(sides[len(sides) - 1 - index][4])
        def _():
            copy_to(index).wait_recv()


def leaf_kernel(cols_y, leaves, leaf_z, dense, own_in, keep, wrows, grad, kacc, patches):
    step = pl.program_id(0)
    edge, width = own_in.shape[3:]
    depth = dense.shape[0]
    wide = edge + 2
    plane = edge * edge
    rows = edge * plane

    @pl.when(step == 0)
    def _():
        kacc[...] = jnp.zeros_like(kacc)

    height = leaf_z[step]
    column = step // leaves
    x0 = (column // cols_y) * edge
    y0 = (column % cols_y) * edge

    @pl.when(height < 0)
    def _():
        grad[...] = jnp.zeros_like(grad)

    @pl.when(height >= 0)
    def _():
        def window(position):
            block = dense[position, pl.ds(x0, wide), pl.ds(y0, wide)]
            return block.astype(F32).reshape(wide * wide, edge, width)

        mid = window(height)
        low = window(jnp.maximum(height - 1, 0))
        low = jnp.where(height > 0, low, jnp.zeros_like(low))
        high = window(jnp.minimum(height + 1, depth - 1))
        high = jnp.where(height < depth - 1, high, jnp.zeros_like(high))
        spot = lax.broadcasted_iota(jnp.int32, low.shape, 1)
        shifted = (
            jnp.where(spot == edge - 1, pltpu.roll(high, edge - 1, 1), pltpu.roll(mid, edge - 1, 1)),
            mid,
            jnp.where(spot == 0, pltpu.roll(low, 1, 1), pltpu.roll(mid, 1, 1)),
        )
        for c in range(3):
            cells = shifted[c].reshape(wide, wide, edge, width)
            for b in range(3):
                piece = cells[:, 2 - b : 2 - b + edge].reshape(wide * plane, width)
                lane = (3 * b + c) * width
                patches[:, lane : lane + width] = piece.astype(BF16)
        kept = jnp.broadcast_to(keep[0], (width, rows))
        own = own_in[:, :, 0].astype(F32).reshape(rows, width)
        own_t = (own.T * kept).astype(BF16)
        result = jnp.zeros((rows, width), F32)
        for a in range(3):
            columns = patches[(2 - a) * plane : (2 - a) * plane + rows, :]
            result += jnp.dot(
                columns,
                wrows[9 * a * width : 9 * (a + 1) * width, :],
                preferred_element_type=F32,
            )
            terms = jnp.dot(own_t, columns, preferred_element_type=F32)
            for j in range(9):
                row = (9 * a + j) * width
                kacc[row : row + width, :] += terms[:, j * width : (j + 1) * width]
        result = result * kept.T
        grad[:, :, 0] = result.reshape(edge, edge, edge, width).astype(BF16)


def parts_of(sizes, per):
    n_dcn, n_gx, n_gy = sizes
    second = max(8, int(per * 0.36 / 8 + 0.5) * 8)
    groups = n_gx * n_gy
    return (
        (0, per - second, ("gy", "gx")),
        ((per - second) * groups, second, ("gx", "gy")),
    )


def reduce_kernel(sizes, scale, per, acc, out, half_buf, half_sum, *rest):
    n_dcn, n_gx, n_gy = sizes
    first_buf, first_sum, second_buf = rest[0:2], rest[2:4], rest[4:6]
    send, recv = rest[6:8]
    count = {"dcn": n_dcn, "gx": n_gx, "gy": n_gy}
    here = {name: lax.axis_index(name) for name in count}
    half = per * n_gx * n_gy
    parts = parts_of(sizes, per)

    def peer(axis, d):
        return lax.rem(here[axis] + d, count[axis])

    def device(axis, d):
        return tuple(peer(axis, d) if name == axis else here[name] for name in count)

    barrier = pltpu.get_barrier_semaphore()
    others = [(axis, d) for axis in count for d in range(1, count[axis])]
    for axis, d in others:
        pl.semaphore_signal(barrier, inc=1, device_id=device(axis, d), device_id_type=MESH)
    pl.semaphore_wait(barrier, len(others))

    used = [0]

    def copy(src, dst, axis, d):
        slot = used[0]
        used[0] += 1
        made = pltpu.make_async_remote_copy(
            src_ref=src,
            dst_ref=dst,
            send_sem=send.at[slot],
            recv_sem=recv.at[slot],
            device_id=device(axis, d),
            device_id_type=MESH,
        )
        made.start()
        return made

    def span(start, size):
        return pl.ds(pl.multiple_of(start, 8), size)

    def done(copies):
        for made in copies:
            made.wait()

    mine = here["dcn"] * half
    flights = []
    for start, chunk, order in parts:
        size = chunk * n_gx * n_gy
        flights.append(
            [
                copy(
                    acc.at[span(peer("dcn", d) * half + start, size)],
                    half_buf.at[d - 1, span(start, size)],
                    "dcn",
                    d,
                )
                for d in range(1, n_dcn)
            ]
        )
    for i, (start, chunk, order) in enumerate(parts):
        size = chunk * n_gx * n_gy
        done(flights[i])
        total = acc[span(mine + start, size), :]
        for d in range(1, n_dcn):
            total += half_buf[d - 1, span(start, size), :]
        half_sum[span(start, size), :] = total
        piece = size // count[order[0]]
        flights[i] = [
            copy(
                half_sum.at[span(start + peer(order[0], d) * piece, piece)],
                first_buf[i].at[d - 1],
                order[0],
                d,
            )
            for d in range(1, count[order[0]])
        ]
    for i, (start, chunk, order) in enumerate(parts):
        piece = chunk * count[order[1]]
        done(flights[i])
        total = half_sum[span(start + here[order[0]] * piece, piece), :]
        for d in range(1, count[order[0]]):
            total += first_buf[i][d - 1]
        first_sum[i][...] = total
        flights[i] = [
            copy(
                first_sum[i].at[span(peer(order[1], d) * chunk, chunk)],
                second_buf[i].at[d - 1],
                order[1],
                d,
            )
            for d in range(1, count[order[1]])
        ]
    for i, (start, chunk, order) in enumerate(parts):
        piece = chunk * count[order[1]]
        done(flights[i])
        total = first_sum[i][span(here[order[1]] * chunk, chunk), :]
        for d in range(1, count[order[1]]):
            total += second_buf[i][d - 1]
        spot = span(mine + start + here[order[0]] * piece + here[order[1]] * chunk, chunk)
        out[spot, :] = total * scale
        flights[i] = [
            copy(out.at[spot], out.at[spot], order[1], d) for d in range(1, count[order[1]])
        ]
    last = []
    for i, (start, chunk, order) in enumerate(parts):
        piece = chunk * count[order[1]]
        done(flights[i])
        spot = span(mine + start + here[order[0]] * piece, piece)
        flights[i] = [
            copy(out.at[spot], out.at[spot], order[0], d) for d in range(1, count[order[0]])
        ]
        last += [copy(out.at[spot], out.at[spot], "dcn", d) for d in range(1, n_dcn)]
    for i, (start, chunk, order) in enumerate(parts):
        piece = chunk * count[order[1]]
        for d, made in enumerate(flights[i], 1):
            made.wait()
            origin = lax.rem(here[order[0]] + count[order[0]] - d, count[order[0]])
            spot = span(mine + start + origin * piece, piece)
            last += [copy(out.at[spot], out.at[spot], "dcn", e) for e in range(1, n_dcn)]
    done(last)


def local(features, grad_out, occupancy, leaf_z, neighbours, kernel):
    edge = features.shape[4]
    leaves = features.shape[3]
    width = features.shape[-1]
    cols_x = leaf_z.shape[1]
    cols_y = leaf_z.shape[2]
    depth = 3
    voxels = edge * edge * edge
    sizes = tuple(lax.axis_size(name) for name in ("dcn", "gx", "gy"))
    devices = sizes[0] * sizes[1] * sizes[2]
    slots = cols_x * cols_y * leaves
    nx, ny = cols_x * edge, cols_y * edge
    vmem = pl.BlockSpec(memory_space=pltpu.VMEM)
    limit = 40 * 2**20

    heights = leaf_z.reshape(slots)
    keep = occupancy.reshape(cols_x, edge, cols_y, edge, leaves, edge)
    keep = keep.transpose(0, 2, 4, 1, 3, 5).reshape(slots, 1, voxels).astype(F32)

    dense, wrows = pl.pallas_call(
        functools.partial(halo_kernel, sizes, (cols_x, cols_y)),
        out_shape=[
            jax.ShapeDtypeStruct((depth, nx + 2, ny + 2, edge, width), BF16),
            jax.ShapeDtypeStruct((27 * width, width), BF16),
        ],
        in_specs=[pl.BlockSpec(memory_space=pltpu.SMEM), vmem, vmem, vmem],
        out_specs=[vmem, vmem],
        scratch_shapes=[pltpu.SemaphoreType.DMA((8,)), pltpu.SemaphoreType.DMA((8,))],
        compiler_params=pltpu.CompilerParams(
            collective_id=0, has_side_effects=True, vmem_limit_bytes=limit
        ),
    )(heights, grad_out[0], keep, kernel)

    per = max(16, -(-27 * width // (devices * 8)) * 8)
    total_rows = per * devices

    def whole(*shape):
        return pl.BlockSpec(shape, lambda i, z: (0,) * len(shape))

    def leaf_at(i, z):
        column = i // leaves
        return (column // cols_y, column % cols_y, i % leaves, 0, 0)

    leaf_block = pl.BlockSpec((edge, edge, 1, edge, width), leaf_at)
    block, kacc = pl.pallas_call(
        functools.partial(leaf_kernel, cols_y, leaves),
        grid_spec=pltpu.PrefetchScalarGridSpec(
            num_scalar_prefetch=1,
            grid=(slots,),
            in_specs=[
                whole(*dense.shape),
                leaf_block,
                pl.BlockSpec((1, 1, voxels), lambda i, z: (i, 0, 0)),
                whole(*wrows.shape),
            ],
            out_specs=[leaf_block, whole(total_rows, width)],
            scratch_shapes=[pltpu.VMEM(((edge + 2) * edge * edge, 9 * width), BF16)],
        ),
        out_shape=[
            jax.ShapeDtypeStruct((nx, ny, leaves, edge, width), BF16),
            jax.ShapeDtypeStruct((total_rows, width), F32),
        ],
        compiler_params=pltpu.CompilerParams(vmem_limit_bytes=limit),
        cost_estimate=pl.CostEstimate(
            flops=4 * slots * voxels * 27 * width * width,
            bytes_accessed=8 * 2**20,
            transcendentals=0,
        ),
    )(heights, dense, features[0], keep, wrows)

    scale = 1.0 / math.sqrt(devices * cols_x * cols_y * voxels * leaves)
    half = total_rows // sizes[0]
    count = {"gx": sizes[1], "gy": sizes[2]}
    parts = parts_of(sizes, per)
    copies = 2 * (sizes[0] - 1) + 4 * (sizes[1] + sizes[2] - 2)
    copies += (sizes[0] - 1) * (sizes[1] + sizes[2])
    kernel_grad = pl.pallas_call(
        functools.partial(reduce_kernel, sizes, scale, per),
        out_shape=jax.ShapeDtypeStruct((total_rows, width), F32),
        in_specs=[vmem],
        out_specs=vmem,
        scratch_shapes=[
            pltpu.VMEM((sizes[0] - 1, half, width), F32),
            pltpu.VMEM((half, width), F32),
        ]
        + [
            pltpu.VMEM((count[order[0]] - 1, chunk * count[order[1]], width), F32)
            for _, chunk, order in parts
        ]
        + [pltpu.VMEM((chunk * count[order[1]], width), F32) for _, chunk, order in parts]
        + [
            pltpu.VMEM((count[order[1]] - 1, chunk, width), F32) for _, chunk, order in parts
        ]
        + [pltpu.SemaphoreType.DMA((copies,)), pltpu.SemaphoreType.DMA((copies,))],
        compiler_params=pltpu.CompilerParams(
            collective_id=1, has_side_effects=True, vmem_limit_bytes=limit
        ),
    )(kacc)
    kernel_grad = kernel_grad[: 27 * width].reshape(27, width, width)
    return (block[None], kernel_grad)


def solution(mesh):
    return jax.shard_map(
        local,
        mesh=mesh,
        in_specs=(
            P("dcn", "gx", "gy", None, None, None),
            P("dcn", "gx", "gy", None, None, None),
            P("dcn", "gx", "gy", None, None),
            P("dcn", "gx", "gy", None),
            P("dcn", "gx", "gy", None, None),
            P(),
        ),
        out_specs=(P("dcn", "gx", "gy", None, None, None), P()),
        check_vma=False,
    )
```

```python
import functools
import math

import jax
import jax.numpy as jnp
from jax import lax
from jax.experimental import pallas as pl
from jax.experimental.pallas import tpu as pltpu
from jax.sharding import PartitionSpec as P

MESH = pl.DeviceIdType.MESH
BF16 = jnp.bfloat16
F32 = jnp.float32


def sides_of(sizes):
    n_gx, n_gy = sizes[1:]
    gx, gy = lax.axis_index("gx"), lax.axis_index("gy")
    sides = []
    for dx in (-1, 0, 1):
        for dy in (-1, 0, 1):
            if dx or dy:
                x, y = gx + dx, gy + dy
                inside = (x >= 0) & (x < n_gx) & (y >= 0) & (y < n_gy)
                sides.append((dx, dy, x, y, inside))
    return sides


def halo_kernel(sizes, cols, leaf_z, grad_out, keep, kernel, dense, wrows, send, recv):
    cols_x, cols_y = cols
    leaves, edge, width = grad_out.shape[2:]
    depth = dense.shape[0]
    voxels = edge * edge * edge
    extent = (cols_x * edge, cols_y * edge)
    dcn = lax.axis_index("dcn")
    sides = sides_of(sizes)
    barrier = pltpu.get_barrier_semaphore()
    for dx, dy, x, y, inside in sides:

        @pl.when(inside)
        def _():
            pl.semaphore_signal(barrier, inc=1, device_id=(dcn, x, y), device_id_type=MESH)

    for cx in range(cols_x):
        for cy in range(cols_y):
            masked = []
            for leaf in range(leaves):
                slot = (cx * cols_y + cy) * leaves + leaf
                cells = grad_out[
                    cx * edge : (cx + 1) * edge, cy * edge : (cy + 1) * edge, leaf
                ].astype(F32)
                kept = jnp.broadcast_to(keep[slot].astype(F32), (width, voxels)).T
                masked.append((leaf_z[cx, cy, leaf], cells * kept.reshape(edge, edge, edge, width)))
            for z in range(depth):
                placed = sum(
                    jnp.where(height == z, cells, jnp.zeros_like(cells))
                    for height, cells in masked
                )
                dense[
                    z,
                    1 + cx * edge : 1 + (cx + 1) * edge,
                    1 + cy * edge : 1 + (cy + 1) * edge,
                ] = placed.astype(BF16)

    def source(step, size):
        return {-1: pl.ds(1, 1), 0: pl.ds(1, size), 1: pl.ds(size, 1)}[step]

    def target(step, size):
        return {-1: pl.ds(size + 1, 1), 0: pl.ds(1, size), 1: pl.ds(0, 1)}[step]

    def copy_to(index):
        dx, dy, x, y, _ = sides[index]
        return pltpu.make_async_remote_copy(
            src_ref=dense.at[:, source(dx, extent[0]), source(dy, extent[1])],
            dst_ref=dense.at[:, target(dx, extent[0]), target(dy, extent[1])],
            send_sem=send.at[index],
            recv_sem=recv.at[index],
            device_id=(dcn, x, y),
            device_id_type=MESH,
        )

    pl.semaphore_wait(barrier, sum(inside.astype(jnp.int32) for *_, inside in sides))

    for index, (dx, dy, x, y, inside) in enumerate(sides):

        @pl.when(inside)
        def _():
            copy_to(index).start()

        @pl.when(jnp.logical_not(inside))
        def _():
            ends = []
            for step, size in ((dx, extent[0]), (dy, extent[1])):
                ends.append({-1: slice(0, 1), 0: slice(1, size + 1), 1: slice(size + 1, size + 2)}[step])
            spot = dense.at[:, ends[0], ends[1]]
            spot[...] = jnp.zeros(spot.shape, BF16)

    for k in range(kernel.shape[0]):
        row, lane = (k % 9) * width, (k // 9) * width
        wrows[row : row + width, lane : lane + width] = kernel[k].astype(F32).T.astype(BF16)

    for index in range(len(sides)):

        @pl.when(sides[index][4])
        def _():
            copy_to(index).wait_send()

        @pl.when(sides[len(sides) - 1 - index][4])
        def _():
            copy_to(index).wait_recv()


def leaf_kernel(cols_y, leaves, leaf_z, dense, own_in, keep, wrows, grad, kacc, patches):
    step = pl.program_id(0)
    edge, width = own_in.shape[3:]
    depth = dense.shape[0]
    wide = edge + 2
    plane = edge * edge
    rows = edge * plane

    @pl.when(step == 0)
    def _():
        kacc[...] = jnp.zeros_like(kacc)

    column = step // leaves
    height = leaf_z[column // cols_y, column % cols_y, step % leaves]
    x0 = (column // cols_y) * edge
    y0 = (column % cols_y) * edge

    @pl.when(height < 0)
    def _():
        grad[...] = jnp.zeros_like(grad)

    @pl.when(height >= 0)
    def _():
        def window(position):
            block = dense[position, pl.ds(x0, wide), pl.ds(y0, wide)]
            return block.astype(F32).reshape(wide * wide, edge, width)

        mid = window(height)
        low = window(jnp.maximum(height - 1, 0))
        low = jnp.where(height > 0, low, jnp.zeros_like(low))
        high = window(jnp.minimum(height + 1, depth - 1))
        high = jnp.where(height < depth - 1, high, jnp.zeros_like(high))
        spot = lax.broadcasted_iota(jnp.int32, low.shape, 1)
        shifted = (
            jnp.where(spot == edge - 1, pltpu.roll(high, edge - 1, 1), pltpu.roll(mid, edge - 1, 1)),
            mid,
            jnp.where(spot == 0, pltpu.roll(low, 1, 1), pltpu.roll(mid, 1, 1)),
        )
        for c in range(3):
            cells = shifted[c].reshape(wide, wide, edge, width)
            for b in range(3):
                piece = cells[:, 2 - b : 2 - b + edge].reshape(wide * plane, width)
                lane = (3 * b + c) * width
                patches[:, lane : lane + width] = piece.astype(BF16)
        kept = jnp.broadcast_to(keep[0].astype(F32), (width, rows))
        own = own_in[:, :, 0].astype(F32).reshape(rows, width)
        own_t = own.T * kept
        gap = jnp.zeros((width, 2 * plane), F32)
        ahead = jnp.concatenate([own_t, gap], axis=1)
        behind = jnp.concatenate([gap, own_t], axis=1)
        shifted_in = jnp.concatenate([behind, pltpu.roll(ahead, plane, 1), ahead], axis=0).astype(BF16)
        terms = jnp.dot(shifted_in, patches[...], preferred_element_type=F32)
        for a in range(3):
            for j in range(9):
                row = (9 * a + j) * width
                kacc[row : row + width, :] += terms[
                    a * width : (a + 1) * width, j * width : (j + 1) * width
                ]
        sums = jnp.dot(patches[...], wrows[...], preferred_element_type=F32)
        result = sum(
            sums[(2 - a) * plane : (2 - a) * plane + rows, a * width : (a + 1) * width]
            for a in range(3)
        )
        result = result * kept.T
        grad[:, :, 0] = result.reshape(edge, edge, edge, width).astype(BF16)


def parts_of(sizes, per):
    blocks = per // 8
    crossed = max(1, int(blocks * 0.36 + 0.5))
    lengths = []
    for total, order in ((blocks - crossed, ("gy", "gx")), (crossed, ("gx", "gy"))):
        lengths.append([((total + 1) // 2, order), (total // 2, order)])
    start = 0
    parts = []
    for pick in (0, 1):
        for choice in lengths:
            length, order = choice[pick]
            if length:
                parts.append((start, 8 * length, order))
                start += 8 * length * sizes[1] * sizes[2]
    return tuple(parts)


def reduce_kernel(sizes, scale, per, acc, out, half_buf, half_sum, *rest):
    n_dcn, n_gx, n_gy = sizes
    parts = parts_of(sizes, per)
    many = len(parts)
    first_buf, first_sum, second_buf = rest[:many], rest[many : 2 * many], rest[2 * many : 3 * many]
    send, recv = rest[3 * many :]
    count = {"dcn": n_dcn, "gx": n_gx, "gy": n_gy}
    here = {name: lax.axis_index(name) for name in count}
    half = per * n_gx * n_gy

    def peer(axis, d):
        return lax.rem(here[axis] + d, count[axis])

    def device(axis, d):
        return tuple(peer(axis, d) if name == axis else here[name] for name in count)

    barrier = pltpu.get_barrier_semaphore()
    others = [(axis, d) for axis in count for d in range(1, count[axis])]
    for axis, d in others:
        pl.semaphore_signal(barrier, inc=1, device_id=device(axis, d), device_id_type=MESH)
    pl.semaphore_wait(barrier, len(others))

    used = [0]

    def copy(src, dst, axis, d):
        slot = used[0]
        used[0] += 1
        made = pltpu.make_async_remote_copy(
            src_ref=src,
            dst_ref=dst,
            send_sem=send.at[slot],
            recv_sem=recv.at[slot],
            device_id=device(axis, d),
            device_id_type=MESH,
        )
        made.start()
        return made

    def span(start, size):
        return pl.ds(pl.multiple_of(start, 8), size)

    def done(copies):
        for made in copies:
            made.wait()

    mine = here["dcn"] * half
    flights = []
    for start, chunk, order in parts:
        size = chunk * n_gx * n_gy
        flights.append(
            [
                copy(
                    acc.at[span(peer("dcn", d) * half + start, size)],
                    half_buf.at[d - 1, span(start, size)],
                    "dcn",
                    d,
                )
                for d in range(1, n_dcn)
            ]
        )
    for i, (start, chunk, order) in enumerate(parts):
        size = chunk * n_gx * n_gy
        done(flights[i])
        total = acc[span(mine + start, size), :]
        for d in range(1, n_dcn):
            total += half_buf[d - 1, span(start, size), :]
        half_sum[span(start, size), :] = total
        piece = size // count[order[0]]
        flights[i] = [
            copy(
                half_sum.at[span(start + peer(order[0], d) * piece, piece)],
                first_buf[i].at[d - 1],
                order[0],
                d,
            )
            for d in range(1, count[order[0]])
        ]
    for i, (start, chunk, order) in enumerate(parts):
        piece = chunk * count[order[1]]
        done(flights[i])
        total = half_sum[span(start + here[order[0]] * piece, piece), :]
        for d in range(1, count[order[0]]):
            total += first_buf[i][d - 1]
        first_sum[i][...] = total
        flights[i] = [
            copy(
                first_sum[i].at[span(peer(order[1], d) * chunk, chunk)],
                second_buf[i].at[d - 1],
                order[1],
                d,
            )
            for d in range(1, count[order[1]])
        ]
    for i, (start, chunk, order) in enumerate(parts):
        piece = chunk * count[order[1]]
        done(flights[i])
        total = first_sum[i][span(here[order[1]] * chunk, chunk), :]
        for d in range(1, count[order[1]]):
            total += second_buf[i][d - 1]
        spot = span(mine + start + here[order[0]] * piece + here[order[1]] * chunk, chunk)
        out[spot, :] = total * scale
        flights[i] = [
            copy(out.at[spot], out.at[spot], order[1], d) for d in range(1, count[order[1]])
        ]
    last = []
    for i, (start, chunk, order) in enumerate(parts):
        piece = chunk * count[order[1]]
        done(flights[i])
        spot = span(mine + start + here[order[0]] * piece, piece)
        flights[i] = [
            copy(out.at[spot], out.at[spot], order[0], d) for d in range(1, count[order[0]])
        ]
        last += [copy(out.at[spot], out.at[spot], "dcn", d) for d in range(1, n_dcn)]
    for i, (start, chunk, order) in enumerate(parts):
        piece = chunk * count[order[1]]
        for d, made in enumerate(flights[i], 1):
            made.wait()
            origin = lax.rem(here[order[0]] + count[order[0]] - d, count[order[0]])
            spot = span(mine + start + origin * piece, piece)
            last += [copy(out.at[spot], out.at[spot], "dcn", e) for e in range(1, n_dcn)]
    done(last)


def local(features, grad_out, occupancy, leaf_z, neighbours, kernel):
    edge = features.shape[4]
    leaves = features.shape[3]
    width = features.shape[-1]
    cols_x = leaf_z.shape[1]
    cols_y = leaf_z.shape[2]
    depth = 3
    voxels = edge * edge * edge
    sizes = tuple(lax.axis_size(name) for name in ("dcn", "gx", "gy"))
    devices = sizes[0] * sizes[1] * sizes[2]
    slots = cols_x * cols_y * leaves
    nx, ny = cols_x * edge, cols_y * edge
    vmem = pl.BlockSpec(memory_space=pltpu.VMEM)
    limit = 40 * 2**20

    heights = leaf_z[0]
    keep = occupancy.reshape(cols_x, edge, cols_y, edge, leaves, edge)
    keep = keep.transpose(0, 2, 4, 1, 3, 5).reshape(slots, 1, voxels)

    dense, wrows = pl.pallas_call(
        functools.partial(halo_kernel, sizes, (cols_x, cols_y)),
        out_shape=[
            jax.ShapeDtypeStruct((depth, nx + 2, ny + 2, edge, width), BF16),
            jax.ShapeDtypeStruct((9 * width, 3 * width), BF16),
        ],
        in_specs=[pl.BlockSpec(memory_space=pltpu.SMEM), vmem, vmem, vmem],
        out_specs=[vmem, vmem],
        scratch_shapes=[pltpu.SemaphoreType.DMA((8,)), pltpu.SemaphoreType.DMA((8,))],
        compiler_params=pltpu.CompilerParams(
            collective_id=0, has_side_effects=True, vmem_limit_bytes=limit
        ),
    )(heights, grad_out[0], keep, kernel)

    per = max(16, -(-27 * width // (devices * 8)) * 8)
    total_rows = per * devices

    def whole(*shape):
        return pl.BlockSpec(shape, lambda i, z: (0,) * len(shape))

    def leaf_at(i, z):
        column = i // leaves
        return (column // cols_y, column % cols_y, i % leaves, 0, 0)

    leaf_block = pl.BlockSpec((edge, edge, 1, edge, width), leaf_at)
    block, kacc = pl.pallas_call(
        functools.partial(leaf_kernel, cols_y, leaves),
        grid_spec=pltpu.PrefetchScalarGridSpec(
            num_scalar_prefetch=1,
            grid=(slots,),
            in_specs=[
                whole(*dense.shape),
                leaf_block,
                pl.BlockSpec((1, 1, voxels), lambda i, z: (i, 0, 0)),
                whole(*wrows.shape),
            ],
            out_specs=[leaf_block, whole(total_rows, width)],
            scratch_shapes=[pltpu.VMEM(((edge + 2) * edge * edge, 9 * width), BF16)],
        ),
        out_shape=[
            jax.ShapeDtypeStruct((nx, ny, leaves, edge, width), BF16),
            jax.ShapeDtypeStruct((total_rows, width), F32),
        ],
        compiler_params=pltpu.CompilerParams(vmem_limit_bytes=limit),
        cost_estimate=pl.CostEstimate(
            flops=4 * slots * voxels * 27 * width * width,
            bytes_accessed=8 * 2**20,
            transcendentals=0,
        ),
    )(heights, dense, features[0], keep, wrows)

    scale = 1.0 / math.sqrt(devices * cols_x * cols_y * voxels * leaves)
    half = total_rows // sizes[0]
    count = {"gx": sizes[1], "gy": sizes[2]}
    parts = parts_of(sizes, per)
    copies = sum(
        sizes[0] - 1 + 2 * (sizes[1] + sizes[2] - 2) + (sizes[0] - 1) * count[order[0]]
        for _, _, order in parts
    )
    kernel_grad = pl.pallas_call(
        functools.partial(reduce_kernel, sizes, scale, per),
        out_shape=jax.ShapeDtypeStruct((total_rows, width), F32),
        in_specs=[vmem],
        out_specs=vmem,
        scratch_shapes=[
            pltpu.VMEM((sizes[0] - 1, half, width), F32),
            pltpu.VMEM((half, width), F32),
        ]
        + [
            pltpu.VMEM((count[order[0]] - 1, chunk * count[order[1]], width), F32)
            for _, chunk, order in parts
        ]
        + [pltpu.VMEM((chunk * count[order[1]], width), F32) for _, chunk, order in parts]
        + [
            pltpu.VMEM((count[order[1]] - 1, chunk, width), F32) for _, chunk, order in parts
        ]
        + [pltpu.SemaphoreType.DMA((copies,)), pltpu.SemaphoreType.DMA((copies,))],
        compiler_params=pltpu.CompilerParams(
            collective_id=1, has_side_effects=True, vmem_limit_bytes=limit
        ),
    )(kacc)
    kernel_grad = kernel_grad[: 27 * width].reshape(27, width, width)
    return (block[None], kernel_grad)


def solution(mesh):
    return jax.shard_map(
        local,
        mesh=mesh,
        in_specs=(
            P("dcn", "gx", "gy", None, None, None),
            P("dcn", "gx", "gy", None, None, None),
            P("dcn", "gx", "gy", None, None),
            P("dcn", "gx", "gy", None),
            P("dcn", "gx", "gy", None, None),
            P(),
        ),
        out_specs=(P("dcn", "gx", "gy", None, None, None), P()),
        check_vma=False,
    )
```

```python
import functools
import math

import jax
import jax.numpy as jnp
from jax import lax
from jax.experimental import pallas as pl
from jax.experimental.pallas import tpu as pltpu
from jax.sharding import PartitionSpec as P

MESH = pl.DeviceIdType.MESH
BF16 = jnp.bfloat16
F32 = jnp.float32


def sides_of(sizes):
    n_gx, n_gy = sizes[1:]
    gx, gy = lax.axis_index("gx"), lax.axis_index("gy")
    sides = []
    for dx in (-1, 0, 1):
        for dy in (-1, 0, 1):
            if dx or dy:
                x, y = gx + dx, gy + dy
                inside = (x >= 0) & (x < n_gx) & (y >= 0) & (y < n_gy)
                sides.append((dx, dy, x, y, inside))
    return sides


def halo_kernel(
    sizes, cols, leaf_z, keep, grad_far, kernel_far, dense, wrows, grad_out, kernel, near, send, recv
):
    cols_x, cols_y = cols
    leaves, edge, width = grad_out.shape[2:]
    depth = dense.shape[0]
    voxels = edge * edge * edge
    extent = (cols_x * edge, cols_y * edge)
    dcn = lax.axis_index("dcn")
    sides = sides_of(sizes)
    fetch_grad = pltpu.make_async_copy(grad_far, grad_out, near.at[0])
    fetch_kernel = pltpu.make_async_copy(kernel_far, kernel, near.at[1])
    fetch_grad.start()
    fetch_kernel.start()
    barrier = pltpu.get_barrier_semaphore()
    for dx, dy, x, y, inside in sides:

        @pl.when(inside)
        def _():
            pl.semaphore_signal(barrier, inc=1, device_id=(dcn, x, y), device_id_type=MESH)

    fetch_grad.wait()
    for cx in range(cols_x):
        for cy in range(cols_y):
            masked = []
            for leaf in range(leaves):
                slot = (cx * cols_y + cy) * leaves + leaf
                cells = grad_out[
                    cx * edge : (cx + 1) * edge, cy * edge : (cy + 1) * edge, leaf
                ].astype(F32)
                kept = jnp.broadcast_to(keep[slot].astype(F32), (width, voxels)).T
                masked.append((leaf_z[cx, cy, leaf], cells * kept.reshape(edge, edge, edge, width)))
            for z in range(depth):
                placed = sum(
                    jnp.where(height == z, cells, jnp.zeros_like(cells))
                    for height, cells in masked
                )
                dense[
                    z,
                    1 + cx * edge : 1 + (cx + 1) * edge,
                    1 + cy * edge : 1 + (cy + 1) * edge,
                ] = placed.astype(BF16)

    def source(step, size):
        return {-1: pl.ds(1, 1), 0: pl.ds(1, size), 1: pl.ds(size, 1)}[step]

    def target(step, size):
        return {-1: pl.ds(size + 1, 1), 0: pl.ds(1, size), 1: pl.ds(0, 1)}[step]

    def copy_to(index):
        dx, dy, x, y, _ = sides[index]
        return pltpu.make_async_remote_copy(
            src_ref=dense.at[:, source(dx, extent[0]), source(dy, extent[1])],
            dst_ref=dense.at[:, target(dx, extent[0]), target(dy, extent[1])],
            send_sem=send.at[index],
            recv_sem=recv.at[index],
            device_id=(dcn, x, y),
            device_id_type=MESH,
        )

    pl.semaphore_wait(barrier, sum(inside.astype(jnp.int32) for *_, inside in sides))

    for index, (dx, dy, x, y, inside) in enumerate(sides):

        @pl.when(inside)
        def _():
            copy_to(index).start()

        @pl.when(jnp.logical_not(inside))
        def _():
            ends = []
            for step, size in ((dx, extent[0]), (dy, extent[1])):
                ends.append({-1: slice(0, 1), 0: slice(1, size + 1), 1: slice(size + 1, size + 2)}[step])
            spot = dense.at[:, ends[0], ends[1]]
            spot[...] = jnp.zeros(spot.shape, BF16)

    fetch_kernel.wait()
    for k in range(kernel.shape[0]):
        wrows[k * width : (k + 1) * width, :] = kernel[k].astype(F32).T.astype(BF16)

    for index in range(len(sides)):

        @pl.when(sides[index][4])
        def _():
            copy_to(index).wait_send()

        @pl.when(sides[len(sides) - 1 - index][4])
        def _():
            copy_to(index).wait_recv()


def leaf_kernel(leaf_z, dense, features, keep, wrows, grad, kacc, patches):
    cols_x, cols_y, leaves = leaf_z.shape
    edge, width = features.shape[3:]
    depth = dense.shape[0]
    wide = edge + 2
    plane = edge * edge
    rows = edge * plane
    kacc[...] = jnp.zeros_like(kacc)

    @pl.loop(0, cols_x * cols_y * leaves)
    def _(slot):
        column, leaf = slot // leaves, slot % leaves
        cx, cy = column // cols_y, column % cols_y
        height = leaf_z[cx, cy, leaf]
        x0, y0 = cx * edge, cy * edge

        @pl.when(height < 0)
        def _():
            grad[pl.ds(x0, edge), pl.ds(y0, edge), leaf] = jnp.zeros((edge, edge, edge, width), BF16)

        @pl.when(height >= 0)
        def _():
            def window(position):
                block = dense[position, pl.ds(x0, wide), pl.ds(y0, wide)]
                return block.astype(F32).reshape(wide * wide, edge, width)

            mid = window(height)
            low = window(jnp.maximum(height - 1, 0))
            low = jnp.where(height > 0, low, jnp.zeros_like(low))
            high = window(jnp.minimum(height + 1, depth - 1))
            high = jnp.where(height < depth - 1, high, jnp.zeros_like(high))
            spot = lax.broadcasted_iota(jnp.int32, low.shape, 1)
            last = edge - 1
            shifted = (
                jnp.where(spot == last, pltpu.roll(high, last, 1), pltpu.roll(mid, last, 1)),
                mid,
                jnp.where(spot == 0, pltpu.roll(low, 1, 1), pltpu.roll(mid, 1, 1)),
            )
            for c in range(3):
                cells = shifted[c].reshape(wide, wide, edge, width)
                for b in range(3):
                    piece = cells[:, 2 - b : 2 - b + edge].reshape(wide * plane, width)
                    lane = (3 * b + c) * width
                    patches[:, lane : lane + width] = piece.astype(BF16)
            kept = jnp.broadcast_to(keep[slot].astype(F32), (width, rows))
            own = features[pl.ds(x0, edge), pl.ds(y0, edge), leaf].astype(F32)
            own_t = (own.reshape(rows, width).T * kept).astype(BF16)
            result = jnp.zeros((rows, width), F32)
            for a in range(3):
                columns = patches[(2 - a) * plane : (2 - a) * plane + rows, :]
                result += jnp.dot(
                    columns,
                    wrows[9 * a * width : 9 * (a + 1) * width, :],
                    preferred_element_type=F32,
                )
                terms = jnp.dot(own_t, columns, preferred_element_type=F32)
                for j in range(9):
                    row = (9 * a + j) * width
                    kacc[row : row + width, :] += terms[:, j * width : (j + 1) * width]
            result = (result * kept.T).reshape(edge, edge, edge, width)
            grad[pl.ds(x0, edge), pl.ds(y0, edge), leaf] = result.astype(BF16)


def parts_of(sizes, per):
    blocks = per // 8
    crossed = max(1, int(blocks * 0.36 + 0.5))
    lengths = []
    for total, order in ((blocks - crossed, ("gy", "gx")), (crossed, ("gx", "gy"))):
        lengths.append([((total + 1) // 2, order), (total // 2, order)])
    start = 0
    parts = []
    for pick in (0, 1):
        for choice in lengths:
            length, order = choice[pick]
            if length:
                parts.append((start, 8 * length, order))
                start += 8 * length * sizes[1] * sizes[2]
    return tuple(parts)


def reduce_kernel(sizes, scale, per, acc, out, half_buf, half_sum, *rest):
    n_dcn, n_gx, n_gy = sizes
    parts = parts_of(sizes, per)
    many = len(parts)
    first_buf, first_sum, second_buf = rest[:many], rest[many : 2 * many], rest[2 * many : 3 * many]
    send, recv = rest[3 * many :]
    count = {"dcn": n_dcn, "gx": n_gx, "gy": n_gy}
    here = {name: lax.axis_index(name) for name in count}
    half = per * n_gx * n_gy

    def peer(axis, d):
        return lax.rem(here[axis] + d, count[axis])

    def device(axis, d):
        return tuple(peer(axis, d) if name == axis else here[name] for name in count)

    barrier = pltpu.get_barrier_semaphore()
    others = [(axis, d) for axis in count for d in range(1, count[axis])]
    for axis, d in others:
        pl.semaphore_signal(barrier, inc=1, device_id=device(axis, d), device_id_type=MESH)
    pl.semaphore_wait(barrier, len(others))

    used = [0]

    def copy(src, dst, axis, d):
        slot = used[0]
        used[0] += 1
        made = pltpu.make_async_remote_copy(
            src_ref=src,
            dst_ref=dst,
            send_sem=send.at[slot],
            recv_sem=recv.at[slot],
            device_id=device(axis, d),
            device_id_type=MESH,
        )
        made.start()
        return made

    def span(start, size):
        return pl.ds(pl.multiple_of(start, 8), size)

    def done(copies):
        for made in copies:
            made.wait()

    mine = here["dcn"] * half
    flights = []
    for start, chunk, order in parts:
        size = chunk * n_gx * n_gy
        flights.append(
            [
                copy(
                    acc.at[span(peer("dcn", d) * half + start, size)],
                    half_buf.at[d - 1, span(start, size)],
                    "dcn",
                    d,
                )
                for d in range(1, n_dcn)
            ]
        )
    for i, (start, chunk, order) in enumerate(parts):
        size = chunk * n_gx * n_gy
        done(flights[i])
        total = acc[span(mine + start, size), :]
        for d in range(1, n_dcn):
            total += half_buf[d - 1, span(start, size), :]
        half_sum[span(start, size), :] = total
        piece = size // count[order[0]]
        flights[i] = [
            copy(
                half_sum.at[span(start + peer(order[0], d) * piece, piece)],
                first_buf[i].at[d - 1],
                order[0],
                d,
            )
            for d in range(1, count[order[0]])
        ]
    for i, (start, chunk, order) in enumerate(parts):
        piece = chunk * count[order[1]]
        done(flights[i])
        total = half_sum[span(start + here[order[0]] * piece, piece), :]
        for d in range(1, count[order[0]]):
            total += first_buf[i][d - 1]
        first_sum[i][...] = total
        flights[i] = [
            copy(
                first_sum[i].at[span(peer(order[1], d) * chunk, chunk)],
                second_buf[i].at[d - 1],
                order[1],
                d,
            )
            for d in range(1, count[order[1]])
        ]
    for i, (start, chunk, order) in enumerate(parts):
        piece = chunk * count[order[1]]
        done(flights[i])
        total = first_sum[i][span(here[order[1]] * chunk, chunk), :]
        for d in range(1, count[order[1]]):
            total += second_buf[i][d - 1]
        spot = span(mine + start + here[order[0]] * piece + here[order[1]] * chunk, chunk)
        out[spot, :] = total * scale
        flights[i] = [
            copy(out.at[spot], out.at[spot], order[1], d) for d in range(1, count[order[1]])
        ]
    last = []
    for i, (start, chunk, order) in enumerate(parts):
        piece = chunk * count[order[1]]
        done(flights[i])
        spot = span(mine + start + here[order[0]] * piece, piece)
        flights[i] = [
            copy(out.at[spot], out.at[spot], order[0], d) for d in range(1, count[order[0]])
        ]
        last += [copy(out.at[spot], out.at[spot], "dcn", d) for d in range(1, n_dcn)]
    for i, (start, chunk, order) in enumerate(parts):
        piece = chunk * count[order[1]]
        for d, made in enumerate(flights[i], 1):
            made.wait()
            origin = lax.rem(here[order[0]] + count[order[0]] - d, count[order[0]])
            spot = span(mine + start + origin * piece, piece)
            last += [copy(out.at[spot], out.at[spot], "dcn", e) for e in range(1, n_dcn)]
    done(last)


def local(features, grad_out, occupancy, leaf_z, neighbours, kernel):
    edge = features.shape[4]
    leaves = features.shape[3]
    width = features.shape[-1]
    cols_x = leaf_z.shape[1]
    cols_y = leaf_z.shape[2]
    depth = 3
    voxels = edge * edge * edge
    sizes = tuple(lax.axis_size(name) for name in ("dcn", "gx", "gy"))
    devices = sizes[0] * sizes[1] * sizes[2]
    slots = cols_x * cols_y * leaves
    nx, ny = cols_x * edge, cols_y * edge
    vmem = pl.BlockSpec(memory_space=pltpu.VMEM)
    smem = pl.BlockSpec(memory_space=pltpu.SMEM)
    far = pl.BlockSpec(memory_space=pltpu.HBM)
    limit = 40 * 2**20

    heights = leaf_z[0]
    keep = occupancy.reshape(cols_x, edge, cols_y, edge, leaves, edge)
    keep = keep.transpose(0, 2, 4, 1, 3, 5).reshape(slots, 1, voxels)

    dense, wrows = pl.pallas_call(
        functools.partial(halo_kernel, sizes, (cols_x, cols_y)),
        out_shape=[
            jax.ShapeDtypeStruct((depth, nx + 2, ny + 2, edge, width), BF16),
            jax.ShapeDtypeStruct((27 * width, width), BF16),
        ],
        in_specs=[smem, vmem, far, far],
        out_specs=[vmem, vmem],
        scratch_shapes=[
            pltpu.VMEM((nx, ny, leaves, edge, width), BF16),
            pltpu.VMEM(kernel.shape, BF16),
            pltpu.SemaphoreType.DMA((2,)),
            pltpu.SemaphoreType.DMA((8,)),
            pltpu.SemaphoreType.DMA((8,)),
        ],
        compiler_params=pltpu.CompilerParams(
            collective_id=0, has_side_effects=True, vmem_limit_bytes=limit
        ),
    )(heights, keep, grad_out[0], kernel)

    per = max(16, -(-27 * width // (devices * 8)) * 8)
    total_rows = per * devices

    block, kacc = pl.pallas_call(
        leaf_kernel,
        in_specs=[smem, vmem, vmem, vmem, vmem],
        out_specs=[vmem, vmem],
        scratch_shapes=[pltpu.VMEM(((edge + 2) * edge * edge, 9 * width), BF16)],
        out_shape=[
            jax.ShapeDtypeStruct((nx, ny, leaves, edge, width), BF16),
            jax.ShapeDtypeStruct((total_rows, width), F32),
        ],
        compiler_params=pltpu.CompilerParams(vmem_limit_bytes=limit),
        cost_estimate=pl.CostEstimate(
            flops=4 * slots * voxels * 27 * width * width,
            bytes_accessed=8 * 2**20,
            transcendentals=0,
        ),
    )(heights, dense, features[0], keep, wrows)

    scale = 1.0 / math.sqrt(devices * cols_x * cols_y * voxels * leaves)
    half = total_rows // sizes[0]
    count = {"gx": sizes[1], "gy": sizes[2]}
    parts = parts_of(sizes, per)
    copies = sum(
        sizes[0] - 1 + 2 * (sizes[1] + sizes[2] - 2) + (sizes[0] - 1) * count[order[0]]
        for _, _, order in parts
    )
    kernel_grad = pl.pallas_call(
        functools.partial(reduce_kernel, sizes, scale, per),
        out_shape=jax.ShapeDtypeStruct((total_rows, width), F32),
        in_specs=[vmem],
        out_specs=vmem,
        scratch_shapes=[
            pltpu.VMEM((sizes[0] - 1, half, width), F32),
            pltpu.VMEM((half, width), F32),
        ]
        + [
            pltpu.VMEM((count[order[0]] - 1, chunk * count[order[1]], width), F32)
            for _, chunk, order in parts
        ]
        + [pltpu.VMEM((chunk * count[order[1]], width), F32) for _, chunk, order in parts]
        + [
            pltpu.VMEM((count[order[1]] - 1, chunk, width), F32) for _, chunk, order in parts
        ]
        + [pltpu.SemaphoreType.DMA((copies,)), pltpu.SemaphoreType.DMA((copies,))],
        compiler_params=pltpu.CompilerParams(
            collective_id=1, has_side_effects=True, vmem_limit_bytes=limit
        ),
    )(kacc)
    kernel_grad = kernel_grad[: 27 * width].reshape(27, width, width)
    return (block[None], kernel_grad)


def solution(mesh):
    return jax.shard_map(
        local,
        mesh=mesh,
        in_specs=(
            P("dcn", "gx", "gy", None, None, None),
            P("dcn", "gx", "gy", None, None, None),
            P("dcn", "gx", "gy", None, None),
            P("dcn", "gx", "gy", None),
            P("dcn", "gx", "gy", None, None),
            P(),
        ),
        out_specs=(P("dcn", "gx", "gy", None, None, None), P()),
        check_vma=False,
    )
```

```python
import functools
import math

import jax
import jax.numpy as jnp
from jax import lax
from jax.experimental import pallas as pl
from jax.experimental.pallas import tpu as pltpu
from jax.sharding import PartitionSpec as P

MESH = pl.DeviceIdType.MESH
BF16 = jnp.bfloat16
F32 = jnp.float32


def sides_of(sizes):
    n_gx, n_gy = sizes[1:]
    gx, gy = lax.axis_index("gx"), lax.axis_index("gy")
    sides = []
    for dx in (-1, 0, 1):
        for dy in (-1, 0, 1):
            if dx or dy:
                x, y = gx + dx, gy + dy
                inside = (x >= 0) & (x < n_gx) & (y >= 0) & (y < n_gy)
                sides.append((dx, dy, x, y, inside))
    return sides


def halo_kernel(
    sizes, cols, leaf_z, keep, grad_far, kernel_far, dense, wrows, grad_out, kernel, near, send, recv
):
    cols_x, cols_y = cols
    leaves, edge, width = grad_out.shape[2:]
    depth = dense.shape[0]
    voxels = edge * edge * edge
    extent = (cols_x * edge, cols_y * edge)
    dcn = lax.axis_index("dcn")
    sides = sides_of(sizes)
    fetch_grad = pltpu.make_async_copy(grad_far, grad_out, near.at[0])
    fetch_kernel = pltpu.make_async_copy(kernel_far, kernel, near.at[1])
    fetch_grad.start()
    fetch_kernel.start()
    barrier = pltpu.get_barrier_semaphore()
    for dx, dy, x, y, inside in sides:

        @pl.when(inside)
        def _():
            pl.semaphore_signal(barrier, inc=1, device_id=(dcn, x, y), device_id_type=MESH)

    fetch_grad.wait()
    for cx in range(cols_x):
        for cy in range(cols_y):
            masked = []
            for leaf in range(leaves):
                slot = (cx * cols_y + cy) * leaves + leaf
                cells = grad_out[
                    cx * edge : (cx + 1) * edge, cy * edge : (cy + 1) * edge, leaf
                ].astype(F32)
                kept = jnp.broadcast_to(keep[slot].astype(F32), (width, voxels)).T
                masked.append((leaf_z[cx, cy, leaf], cells * kept.reshape(edge, edge, edge, width)))
            for z in range(depth):
                placed = sum(
                    jnp.where(height == z, cells, jnp.zeros_like(cells))
                    for height, cells in masked
                )
                dense[
                    z,
                    1 + cx * edge : 1 + (cx + 1) * edge,
                    1 + cy * edge : 1 + (cy + 1) * edge,
                ] = placed.astype(BF16)

    def source(step, size):
        return {-1: pl.ds(1, 1), 0: pl.ds(1, size), 1: pl.ds(size, 1)}[step]

    def target(step, size):
        return {-1: pl.ds(size + 1, 1), 0: pl.ds(1, size), 1: pl.ds(0, 1)}[step]

    def copy_to(index):
        dx, dy, x, y, _ = sides[index]
        return pltpu.make_async_remote_copy(
            src_ref=dense.at[:, source(dx, extent[0]), source(dy, extent[1])],
            dst_ref=dense.at[:, target(dx, extent[0]), target(dy, extent[1])],
            send_sem=send.at[index],
            recv_sem=recv.at[index],
            device_id=(dcn, x, y),
            device_id_type=MESH,
        )

    pl.semaphore_wait(barrier, sum(inside.astype(jnp.int32) for *_, inside in sides))

    for index, (dx, dy, x, y, inside) in enumerate(sides):

        @pl.when(inside)
        def _():
            copy_to(index).start()

        @pl.when(jnp.logical_not(inside))
        def _():
            ends = []
            for step, size in ((dx, extent[0]), (dy, extent[1])):
                ends.append({-1: slice(0, 1), 0: slice(1, size + 1), 1: slice(size + 1, size + 2)}[step])
            spot = dense.at[:, ends[0], ends[1]]
            spot[...] = jnp.zeros(spot.shape, BF16)

    fetch_kernel.wait()
    for k in range(kernel.shape[0]):
        wrows[k * width : (k + 1) * width, :] = kernel[k].astype(F32).T.astype(BF16)

    for index in range(len(sides)):

        @pl.when(sides[index][4])
        def _():
            copy_to(index).wait_send()

        @pl.when(sides[len(sides) - 1 - index][4])
        def _():
            copy_to(index).wait_recv()


def leaf_kernel(leaf_z, dense, features, keep, wrows, grad, kacc, patches):
    cols_x, cols_y, leaves = leaf_z.shape
    edge, width = features.shape[3:]
    depth = dense.shape[0]
    wide = edge + 2
    plane = edge * edge
    rows = edge * plane
    kacc[...] = jnp.zeros_like(kacc)

    @pl.loop(0, cols_x * cols_y * leaves)
    def _(slot):
        column, leaf = slot // leaves, slot % leaves
        cx, cy = column // cols_y, column % cols_y
        height = leaf_z[cx, cy, leaf]
        x0, y0 = cx * edge, cy * edge

        @pl.when(height < 0)
        def _():
            grad[pl.ds(x0, edge), pl.ds(y0, edge), leaf] = jnp.zeros((edge, edge, edge, width), BF16)

        @pl.when(height >= 0)
        def _():
            def window(position):
                block = dense[position, pl.ds(x0, wide), pl.ds(y0, wide)]
                return block.astype(F32).reshape(wide * wide, edge, width)

            mid = window(height)
            low = window(jnp.maximum(height - 1, 0))
            low = jnp.where(height > 0, low, jnp.zeros_like(low))
            high = window(jnp.minimum(height + 1, depth - 1))
            high = jnp.where(height < depth - 1, high, jnp.zeros_like(high))
            spot = lax.broadcasted_iota(jnp.int32, low.shape, 1)
            last = edge - 1
            shifted = (
                jnp.where(spot == last, pltpu.roll(high, last, 1), pltpu.roll(mid, last, 1)),
                mid,
                jnp.where(spot == 0, pltpu.roll(low, 1, 1), pltpu.roll(mid, 1, 1)),
            )
            for c in range(3):
                cells = shifted[c].reshape(wide, wide, edge, width)
                for b in range(3):
                    piece = cells[:, 2 - b : 2 - b + edge].reshape(wide * plane, width)
                    lane = (3 * b + c) * width
                    patches[:, lane : lane + width] = piece.astype(BF16)
            kept = jnp.broadcast_to(keep[slot].astype(F32), (width, rows))
            own = features[pl.ds(x0, edge), pl.ds(y0, edge), leaf].astype(F32)
            own_t = (own.reshape(rows, width).T * kept).astype(BF16)
            result = jnp.zeros((rows, width), F32)
            for a in range(3):
                columns = patches[(2 - a) * plane : (2 - a) * plane + rows, :]
                result += jnp.dot(
                    columns,
                    wrows[9 * a * width : 9 * (a + 1) * width, :],
                    preferred_element_type=F32,
                )
                terms = jnp.dot(own_t, columns, preferred_element_type=F32)
                for j in range(9):
                    row = (9 * a + j) * width
                    kacc[row : row + width, :] += terms[:, j * width : (j + 1) * width]
            result = (result * kept.T).reshape(edge, edge, edge, width)
            grad[pl.ds(x0, edge), pl.ds(y0, edge), leaf] = result.astype(BF16)


def parts_of(sizes, per):
    blocks = per // 8
    crossed = max(1, int(blocks * 0.36 + 0.5))
    lengths = []
    for total, order in ((blocks - crossed, ("gy", "low", "high")), (crossed, ("low", "high", "gy"))):
        lengths.append([((total + 1) // 2, order), (total // 2, order)])
    start = 0
    parts = []
    for pick in (0, 1):
        for choice in lengths:
            length, order = choice[pick]
            if length:
                parts.append((start, 8 * length, order))
                start += 8 * length * sizes[1] * sizes[2]
    return tuple(parts)


def counts_of(sizes):
    low = 2 if sizes[1] % 2 == 0 else 1
    return {"dcn": sizes[0], "gy": sizes[2], "low": low, "high": sizes[1] // low}


def reduce_kernel(sizes, scale, per, acc, out, half_buf, *rest):
    count = counts_of(sizes)
    gx = lax.axis_index("gx")
    here = {
        "dcn": lax.axis_index("dcn"),
        "gy": lax.axis_index("gy"),
        "low": lax.rem(gx, count["low"]),
        "high": gx // count["low"],
    }
    half = per * sizes[1] * sizes[2]
    parts = parts_of(sizes, per)
    many = 3 * len(parts)
    bufs, sums = rest[:many], rest[many : 2 * many]
    send, recv = rest[2 * many :]

    def peer(axis, d):
        return lax.rem(here[axis] + d, count[axis])

    def device(axis, d):
        at = dict(here)
        at[axis] = peer(axis, d)
        return (at["dcn"], at["high"] * count["low"] + at["low"], at["gy"])

    barrier = pltpu.get_barrier_semaphore()
    others = [(axis, d) for axis in count for d in range(1, count[axis])]
    for axis, d in others:
        pl.semaphore_signal(barrier, inc=1, device_id=device(axis, d), device_id_type=MESH)
    pl.semaphore_wait(barrier, len(others))

    used = [0]

    def copy(src, dst, axis, d):
        slot = used[0]
        used[0] += 1
        made = pltpu.make_async_remote_copy(
            src_ref=src,
            dst_ref=dst,
            send_sem=send.at[slot],
            recv_sem=recv.at[slot],
            device_id=device(axis, d),
            device_id_type=MESH,
        )
        made.start()
        return made

    def span(start, size):
        return pl.ds(pl.multiple_of(start, 8), size)

    def done(copies):
        for made in copies:
            made.wait()

    mine = here["dcn"] * half
    flights = []
    lengths = []
    for start, chunk, order in parts:
        size = chunk * sizes[1] * sizes[2]
        steps = [size]
        for axis in order:
            steps.append(steps[-1] // count[axis])
        lengths.append(steps)
        flights.append(
            [
                copy(
                    acc.at[span(peer("dcn", d) * half + start, size)],
                    half_buf.at[d - 1, span(start, size)],
                    "dcn",
                    d,
                )
                for d in range(1, count["dcn"])
            ]
        )
    for stage in range(4):
        for i, (start, chunk, order) in enumerate(parts):
            size = lengths[i][stage]
            done(flights[i])
            if stage == 0:
                total = acc[span(mine + start, size), :]
                for d in range(1, count["dcn"]):
                    total += half_buf[d - 1, span(start, size), :]
            else:
                axis = order[stage - 1]
                total = sums[3 * i + stage - 1][span(here[axis] * size, size), :]
                for d in range(1, count[axis]):
                    total += bufs[3 * i + stage - 1][d - 1]
            if stage < 3:
                axis, piece = order[stage], lengths[i][stage + 1]
                held = sums[3 * i + stage]
                held[...] = total
                flights[i] = [
                    copy(
                        held.at[span(peer(axis, d) * piece, piece)],
                        bufs[3 * i + stage].at[d - 1],
                        axis,
                        d,
                    )
                    for d in range(1, count[axis])
                ]
            else:
                spot = mine + start
                for axis, length in zip(order, lengths[i][1:]):
                    spot += here[axis] * length
                spot = span(spot, size)
                out[spot, :] = total * scale
                flights[i] = [
                    copy(out.at[spot], out.at[spot], order[2], d)
                    for d in range(1, count[order[2]])
                ]
    last = []
    for stage in (1, 0):
        for i, (start, chunk, order) in enumerate(parts):
            done(flights[i])
            spot = mine + start
            for axis, length in zip(order[: stage + 1], lengths[i][1:]):
                spot += here[axis] * length
            spot = span(spot, lengths[i][stage + 1])
            axis = order[stage]
            flights[i] = [
                copy(out.at[spot], out.at[spot], axis, d) for d in range(1, count[axis])
            ]
            if stage == 0:
                last += [copy(out.at[spot], out.at[spot], "dcn", d) for d in range(1, count["dcn"])]
    for i, (start, chunk, order) in enumerate(parts):
        axis, piece = order[0], lengths[i][1]
        for d, made in enumerate(flights[i], 1):
            made.wait()
            origin = lax.rem(here[axis] + count[axis] - d, count[axis])
            spot = span(mine + start + origin * piece, piece)
            last += [copy(out.at[spot], out.at[spot], "dcn", e) for e in range(1, count["dcn"])]
    done(last)


def local(features, grad_out, occupancy, leaf_z, neighbours, kernel):
    edge = features.shape[4]
    leaves = features.shape[3]
    width = features.shape[-1]
    cols_x = leaf_z.shape[1]
    cols_y = leaf_z.shape[2]
    depth = 3
    voxels = edge * edge * edge
    sizes = tuple(lax.axis_size(name) for name in ("dcn", "gx", "gy"))
    devices = sizes[0] * sizes[1] * sizes[2]
    slots = cols_x * cols_y * leaves
    nx, ny = cols_x * edge, cols_y * edge
    vmem = pl.BlockSpec(memory_space=pltpu.VMEM)
    smem = pl.BlockSpec(memory_space=pltpu.SMEM)
    far = pl.BlockSpec(memory_space=pltpu.HBM)
    limit = 40 * 2**20

    heights = leaf_z[0]
    keep = occupancy.reshape(cols_x, edge, cols_y, edge, leaves, edge)
    keep = keep.transpose(0, 2, 4, 1, 3, 5).reshape(slots, 1, voxels)

    dense, wrows = pl.pallas_call(
        functools.partial(halo_kernel, sizes, (cols_x, cols_y)),
        out_shape=[
            jax.ShapeDtypeStruct((depth, nx + 2, ny + 2, edge, width), BF16),
            jax.ShapeDtypeStruct((27 * width, width), BF16),
        ],
        in_specs=[smem, vmem, far, far],
        out_specs=[vmem, vmem],
        scratch_shapes=[
            pltpu.VMEM((nx, ny, leaves, edge, width), BF16),
            pltpu.VMEM(kernel.shape, BF16),
            pltpu.SemaphoreType.DMA((2,)),
            pltpu.SemaphoreType.DMA((8,)),
            pltpu.SemaphoreType.DMA((8,)),
        ],
        compiler_params=pltpu.CompilerParams(
            collective_id=0, has_side_effects=True, vmem_limit_bytes=limit
        ),
    )(heights, keep, grad_out[0], kernel)

    per = max(16, -(-27 * width // (devices * 8)) * 8)
    total_rows = per * devices

    block, kacc = pl.pallas_call(
        leaf_kernel,
        in_specs=[smem, vmem, vmem, vmem, vmem],
        out_specs=[vmem, vmem],
        scratch_shapes=[pltpu.VMEM(((edge + 2) * edge * edge, 9 * width), BF16)],
        out_shape=[
            jax.ShapeDtypeStruct((nx, ny, leaves, edge, width), BF16),
            jax.ShapeDtypeStruct((total_rows, width), F32),
        ],
        compiler_params=pltpu.CompilerParams(vmem_limit_bytes=limit),
        cost_estimate=pl.CostEstimate(
            flops=4 * slots * voxels * 27 * width * width,
            bytes_accessed=8 * 2**20,
            transcendentals=0,
        ),
    )(heights, dense, features[0], keep, wrows)

    scale = 1.0 / math.sqrt(devices * cols_x * cols_y * voxels * leaves)
    half = total_rows // sizes[0]
    count = counts_of(sizes)
    copies = 0
    bufs, sums = [], []
    for _, chunk, order in parts_of(sizes, per):
        size = chunk * sizes[1] * sizes[2]
        for axis in order:
            sums.append(pltpu.VMEM((size, width), F32))
            size //= count[axis]
            bufs.append(pltpu.VMEM((max(1, count[axis] - 1), size, width), F32))
            copies += 2 * (count[axis] - 1)
        copies += (sizes[0] - 1) * (1 + count[order[0]])
    kernel_grad = pl.pallas_call(
        functools.partial(reduce_kernel, sizes, scale, per),
        out_shape=jax.ShapeDtypeStruct((total_rows, width), F32),
        in_specs=[vmem],
        out_specs=vmem,
        scratch_shapes=[
            pltpu.VMEM((sizes[0] - 1, half, width), F32),
        ]
        + bufs
        + sums
        + [pltpu.SemaphoreType.DMA((copies,)), pltpu.SemaphoreType.DMA((copies,))],
        compiler_params=pltpu.CompilerParams(
            collective_id=1, has_side_effects=True, vmem_limit_bytes=limit
        ),
    )(kacc)
    kernel_grad = kernel_grad[: 27 * width].reshape(27, width, width)
    return (block[None], kernel_grad)


def solution(mesh):
    return jax.shard_map(
        local,
        mesh=mesh,
        in_specs=(
            P("dcn", "gx", "gy", None, None, None),
            P("dcn", "gx", "gy", None, None, None),
            P("dcn", "gx", "gy", None, None),
            P("dcn", "gx", "gy", None),
            P("dcn", "gx", "gy", None, None),
            P(),
        ),
        out_specs=(P("dcn", "gx", "gy", None, None, None), P()),
        check_vma=False,
    )
```

```python
import functools
import math

import jax
import jax.numpy as jnp
from jax import lax
from jax.experimental import pallas as pl
from jax.experimental.pallas import tpu as pltpu
from jax.sharding import PartitionSpec as P

MESH = pl.DeviceIdType.MESH
BF16 = jnp.bfloat16
F32 = jnp.float32


def sides_of(sizes):
    n_gx, n_gy = sizes[1:]
    gx, gy = lax.axis_index("gx"), lax.axis_index("gy")
    sides = []
    for dx in (-1, 0, 1):
        for dy in (-1, 0, 1):
            if dx or dy:
                x, y = gx + dx, gy + dy
                inside = (x >= 0) & (x < n_gx) & (y >= 0) & (y < n_gy)
                sides.append((dx, dy, x, y, inside))
    return sides


def halo_kernel(
    sizes, cols, leaf_z, keep, grad_far, dense, grad_out, near, send, recv
):
    cols_x, cols_y = cols
    leaves, edge, width = grad_out.shape[2:]
    depth = dense.shape[0]
    voxels = edge * edge * edge
    extent = (cols_x * edge, cols_y * edge)
    dcn = lax.axis_index("dcn")
    sides = sides_of(sizes)
    fetch_grad = pltpu.make_async_copy(grad_far, grad_out, near.at[0])
    fetch_grad.start()
    barrier = pltpu.get_barrier_semaphore()
    for dx, dy, x, y, inside in sides:

        @pl.when(inside)
        def _():
            pl.semaphore_signal(barrier, inc=1, device_id=(dcn, x, y), device_id_type=MESH)

    fetch_grad.wait()
    for cx in range(cols_x):
        for cy in range(cols_y):
            masked = []
            for leaf in range(leaves):
                slot = (cx * cols_y + cy) * leaves + leaf
                cells = grad_out[
                    cx * edge : (cx + 1) * edge, cy * edge : (cy + 1) * edge, leaf
                ].astype(F32)
                kept = jnp.broadcast_to(keep[slot].astype(F32), (width, voxels)).T
                masked.append((leaf_z[cx, cy, leaf], cells * kept.reshape(edge, edge, edge, width)))
            for z in range(depth):
                placed = sum(
                    jnp.where(height == z, cells, jnp.zeros_like(cells))
                    for height, cells in masked
                )
                dense[
                    z,
                    1 + cx * edge : 1 + (cx + 1) * edge,
                    1 + cy * edge : 1 + (cy + 1) * edge,
                ] = placed.astype(BF16)

    def source(step, size):
        return {-1: pl.ds(1, 1), 0: pl.ds(1, size), 1: pl.ds(size, 1)}[step]

    def target(step, size):
        return {-1: pl.ds(size + 1, 1), 0: pl.ds(1, size), 1: pl.ds(0, 1)}[step]

    def copy_to(index):
        dx, dy, x, y, _ = sides[index]
        return pltpu.make_async_remote_copy(
            src_ref=dense.at[:, source(dx, extent[0]), source(dy, extent[1])],
            dst_ref=dense.at[:, target(dx, extent[0]), target(dy, extent[1])],
            send_sem=send.at[index],
            recv_sem=recv.at[index],
            device_id=(dcn, x, y),
            device_id_type=MESH,
        )

    pl.semaphore_wait(barrier, sum(inside.astype(jnp.int32) for *_, inside in sides))

    for index, (dx, dy, x, y, inside) in enumerate(sides):

        @pl.when(inside)
        def _():
            copy_to(index).start()

        @pl.when(jnp.logical_not(inside))
        def _():
            ends = []
            for step, size in ((dx, extent[0]), (dy, extent[1])):
                ends.append({-1: slice(0, 1), 0: slice(1, size + 1), 1: slice(size + 1, size + 2)}[step])
            spot = dense.at[:, ends[0], ends[1]]
            spot[...] = jnp.zeros(spot.shape, BF16)

    for index in range(len(sides)):

        @pl.when(sides[index][4])
        def _():
            copy_to(index).wait_send()

        @pl.when(sides[len(sides) - 1 - index][4])
        def _():
            copy_to(index).wait_recv()


def leaf_kernel(leaf_z, dense, features, keep, kernel, grad, kacc, patches, wrows):
    cols_x, cols_y, leaves = leaf_z.shape
    edge, width = features.shape[3:]
    depth = dense.shape[0]
    wide = edge + 2
    plane = edge * edge
    rows = edge * plane
    kacc[...] = jnp.zeros_like(kacc)
    for k in range(kernel.shape[0]):
        wrows[k * width : (k + 1) * width, :] = kernel[k].astype(F32).T.astype(BF16)

    @pl.loop(0, cols_x * cols_y * leaves)
    def _(slot):
        column, leaf = slot // leaves, slot % leaves
        cx, cy = column // cols_y, column % cols_y
        height = leaf_z[cx, cy, leaf]
        x0, y0 = cx * edge, cy * edge

        @pl.when(height < 0)
        def _():
            grad[pl.ds(x0, edge), pl.ds(y0, edge), leaf] = jnp.zeros((edge, edge, edge, width), BF16)

        @pl.when(height >= 0)
        def _():
            def window(position):
                block = dense[position, pl.ds(x0, wide), pl.ds(y0, wide)]
                return block.astype(F32).reshape(wide * wide, edge, width)

            mid = window(height)
            low = window(jnp.maximum(height - 1, 0))
            low = jnp.where(height > 0, low, jnp.zeros_like(low))
            high = window(jnp.minimum(height + 1, depth - 1))
            high = jnp.where(height < depth - 1, high, jnp.zeros_like(high))
            spot = lax.broadcasted_iota(jnp.int32, low.shape, 1)
            last = edge - 1
            shifted = (
                jnp.where(spot == last, pltpu.roll(high, last, 1), pltpu.roll(mid, last, 1)),
                mid,
                jnp.where(spot == 0, pltpu.roll(low, 1, 1), pltpu.roll(mid, 1, 1)),
            )
            for c in range(3):
                cells = shifted[c].reshape(wide, wide, edge, width)
                for b in range(3):
                    piece = cells[:, 2 - b : 2 - b + edge].reshape(wide * plane, width)
                    lane = (3 * b + c) * width
                    patches[:, lane : lane + width] = piece.astype(BF16)
            kept = jnp.broadcast_to(keep[slot].astype(F32), (width, rows))
            own = features[pl.ds(x0, edge), pl.ds(y0, edge), leaf].astype(F32)
            own_t = (own.reshape(rows, width).T * kept).astype(BF16)
            result = jnp.zeros((rows, width), F32)
            for a in range(3):
                columns = patches[(2 - a) * plane : (2 - a) * plane + rows, :]
                result += jnp.dot(
                    columns,
                    wrows[9 * a * width : 9 * (a + 1) * width, :],
                    preferred_element_type=F32,
                )
                terms = jnp.dot(own_t, columns, preferred_element_type=F32)
                for j in range(9):
                    row = (9 * a + j) * width
                    kacc[row : row + width, :] += terms[:, j * width : (j + 1) * width]
            result = (result * kept.T).reshape(edge, edge, edge, width)
            grad[pl.ds(x0, edge), pl.ds(y0, edge), leaf] = result.astype(BF16)


def parts_of(sizes, per):
    blocks = per // 8
    crossed = max(1, int(blocks * 0.29 + 0.5))
    lengths = []
    for total, order in ((blocks - crossed, ("gy", "gx")), (crossed, ("gx", "gy"))):
        lengths.append([((total + 1) // 2, order), (total // 2, order)])
    start = 0
    parts = []
    for pick in (0, 1):
        for choice in lengths:
            length, order = choice[pick]
            if length:
                parts.append((start, 8 * length, order))
                start += 8 * length * sizes[1] * sizes[2]
    return tuple(parts)


def reduce_kernel(sizes, scale, per, acc, out, half_buf, half_sum, *rest):
    n_dcn, n_gx, n_gy = sizes
    parts = parts_of(sizes, per)
    many = len(parts)
    first_buf, first_sum, second_buf = rest[:many], rest[many : 2 * many], rest[2 * many : 3 * many]
    send, recv = rest[3 * many :]
    count = {"dcn": n_dcn, "gx": n_gx, "gy": n_gy}
    here = {name: lax.axis_index(name) for name in count}
    half = per * n_gx * n_gy

    def peer(axis, d):
        return lax.rem(here[axis] + d, count[axis])

    def device(axis, d):
        return tuple(peer(axis, d) if name == axis else here[name] for name in count)

    barrier = pltpu.get_barrier_semaphore()
    others = [(axis, d) for axis in count for d in range(1, count[axis])]
    for axis, d in others:
        pl.semaphore_signal(barrier, inc=1, device_id=device(axis, d), device_id_type=MESH)
    pl.semaphore_wait(barrier, len(others))

    used = [0]

    def copy(src, dst, axis, d):
        slot = used[0]
        used[0] += 1
        made = pltpu.make_async_remote_copy(
            src_ref=src,
            dst_ref=dst,
            send_sem=send.at[slot],
            recv_sem=recv.at[slot],
            device_id=device(axis, d),
            device_id_type=MESH,
        )
        made.start()
        return made

    def span(start, size):
        return pl.ds(pl.multiple_of(start, 8), size)

    def done(copies):
        for made in copies:
            made.wait()

    mine = here["dcn"] * half
    flights = []
    for start, chunk, order in parts:
        size = chunk * n_gx * n_gy
        flights.append(
            [
                copy(
                    acc.at[span(peer("dcn", d) * half + start, size)],
                    half_buf.at[d - 1, span(start, size)],
                    "dcn",
                    d,
                )
                for d in range(1, n_dcn)
            ]
        )
    for i, (start, chunk, order) in enumerate(parts):
        size = chunk * n_gx * n_gy
        done(flights[i])
        total = acc[span(mine + start, size), :]
        for d in range(1, n_dcn):
            total += half_buf[d - 1, span(start, size), :]
        half_sum[span(start, size), :] = total
        piece = size // count[order[0]]
        flights[i] = [
            copy(
                half_sum.at[span(start + peer(order[0], d) * piece, piece)],
                first_buf[i].at[d - 1],
                order[0],
                d,
            )
            for d in range(1, count[order[0]])
        ]
    for i, (start, chunk, order) in enumerate(parts):
        piece = chunk * count[order[1]]
        done(flights[i])
        total = half_sum[span(start + here[order[0]] * piece, piece), :]
        for d in range(1, count[order[0]]):
            total += first_buf[i][d - 1]
        first_sum[i][...] = total
        flights[i] = [
            copy(
                first_sum[i].at[span(peer(order[1], d) * chunk, chunk)],
                second_buf[i].at[d - 1],
                order[1],
                d,
            )
            for d in range(1, count[order[1]])
        ]
    for i, (start, chunk, order) in enumerate(parts):
        piece = chunk * count[order[1]]
        done(flights[i])
        total = first_sum[i][span(here[order[1]] * chunk, chunk), :]
        for d in range(1, count[order[1]]):
            total += second_buf[i][d - 1]
        spot = span(mine + start + here[order[0]] * piece + here[order[1]] * chunk, chunk)
        out[spot, :] = total * scale
        flights[i] = [
            copy(out.at[spot], out.at[spot], order[1], d) for d in range(1, count[order[1]])
        ]
    last = []
    for i, (start, chunk, order) in enumerate(parts):
        piece = chunk * count[order[1]]
        done(flights[i])
        spot = span(mine + start + here[order[0]] * piece, piece)
        flights[i] = [
            copy(out.at[spot], out.at[spot], order[0], d) for d in range(1, count[order[0]])
        ]
        last += [copy(out.at[spot], out.at[spot], "dcn", d) for d in range(1, n_dcn)]
    for i, (start, chunk, order) in enumerate(parts):
        piece = chunk * count[order[1]]
        for d, made in enumerate(flights[i], 1):
            made.wait()
            origin = lax.rem(here[order[0]] + count[order[0]] - d, count[order[0]])
            spot = span(mine + start + origin * piece, piece)
            last += [copy(out.at[spot], out.at[spot], "dcn", e) for e in range(1, n_dcn)]
    done(last)


def local(features, grad_out, occupancy, leaf_z, neighbours, kernel):
    edge = features.shape[4]
    leaves = features.shape[3]
    width = features.shape[-1]
    cols_x = leaf_z.shape[1]
    cols_y = leaf_z.shape[2]
    depth = 3
    voxels = edge * edge * edge
    sizes = tuple(lax.axis_size(name) for name in ("dcn", "gx", "gy"))
    devices = sizes[0] * sizes[1] * sizes[2]
    slots = cols_x * cols_y * leaves
    nx, ny = cols_x * edge, cols_y * edge
    vmem = pl.BlockSpec(memory_space=pltpu.VMEM)
    smem = pl.BlockSpec(memory_space=pltpu.SMEM)
    far = pl.BlockSpec(memory_space=pltpu.HBM)
    limit = 40 * 2**20

    heights = leaf_z[0]
    keep = occupancy.reshape(cols_x, edge, cols_y, edge, leaves, edge)
    keep = keep.transpose(0, 2, 4, 1, 3, 5).reshape(slots, 1, voxels)

    dense = pl.pallas_call(
        functools.partial(halo_kernel, sizes, (cols_x, cols_y)),
        out_shape=jax.ShapeDtypeStruct((depth, nx + 2, ny + 2, edge, width), BF16),
        in_specs=[smem, vmem, far],
        out_specs=vmem,
        scratch_shapes=[
            pltpu.VMEM((nx, ny, leaves, edge, width), BF16),
            pltpu.SemaphoreType.DMA((1,)),
            pltpu.SemaphoreType.DMA((8,)),
            pltpu.SemaphoreType.DMA((8,)),
        ],
        compiler_params=pltpu.CompilerParams(
            collective_id=0, has_side_effects=True, vmem_limit_bytes=limit
        ),
    )(heights, keep, grad_out[0])

    per = max(16, -(-27 * width // (devices * 8)) * 8)
    total_rows = per * devices

    block, kacc = pl.pallas_call(
        leaf_kernel,
        in_specs=[smem, vmem, vmem, vmem, vmem],
        out_specs=[vmem, vmem],
        scratch_shapes=[
            pltpu.VMEM(((edge + 2) * edge * edge, 9 * width), BF16),
            pltpu.VMEM((27 * width, width), BF16),
        ],
        out_shape=[
            jax.ShapeDtypeStruct((nx, ny, leaves, edge, width), BF16),
            jax.ShapeDtypeStruct((total_rows, width), F32),
        ],
        compiler_params=pltpu.CompilerParams(vmem_limit_bytes=limit),
        cost_estimate=pl.CostEstimate(
            flops=4 * slots * voxels * 27 * width * width,
            bytes_accessed=8 * 2**20,
            transcendentals=0,
        ),
    )(heights, dense, features[0], keep, kernel)

    scale = 1.0 / math.sqrt(devices * cols_x * cols_y * voxels * leaves)
    half = total_rows // sizes[0]
    count = {"gx": sizes[1], "gy": sizes[2]}
    parts = parts_of(sizes, per)
    copies = sum(
        sizes[0] - 1 + 2 * (sizes[1] + sizes[2] - 2) + (sizes[0] - 1) * count[order[0]]
        for _, _, order in parts
    )
    kernel_grad = pl.pallas_call(
        functools.partial(reduce_kernel, sizes, scale, per),
        out_shape=jax.ShapeDtypeStruct((total_rows, width), F32),
        in_specs=[vmem],
        out_specs=vmem,
        scratch_shapes=[
            pltpu.VMEM((sizes[0] - 1, half, width), F32),
            pltpu.VMEM((half, width), F32),
        ]
        + [
            pltpu.VMEM((count[order[0]] - 1, chunk * count[order[1]], width), F32)
            for _, chunk, order in parts
        ]
        + [pltpu.VMEM((chunk * count[order[1]], width), F32) for _, chunk, order in parts]
        + [
            pltpu.VMEM((count[order[1]] - 1, chunk, width), F32) for _, chunk, order in parts
        ]
        + [pltpu.SemaphoreType.DMA((copies,)), pltpu.SemaphoreType.DMA((copies,))],
        compiler_params=pltpu.CompilerParams(
            collective_id=1, has_side_effects=True, vmem_limit_bytes=limit
        ),
    )(kacc)
    kernel_grad = kernel_grad[: 27 * width].reshape(27, width, width)
    return (block[None], kernel_grad)


def solution(mesh):
    return jax.shard_map(
        local,
        mesh=mesh,
        in_specs=(
            P("dcn", "gx", "gy", None, None, None),
            P("dcn", "gx", "gy", None, None, None),
            P("dcn", "gx", "gy", None, None),
            P("dcn", "gx", "gy", None),
            P("dcn", "gx", "gy", None, None),
            P(),
        ),
        out_specs=(P("dcn", "gx", "gy", None, None, None), P()),
        check_vma=False,
    )
```
